128 devices in a mesh: rep: 16 (over z, x_lo, core), shard: 8 (over y, x_hi).
Axes of the slice: x: 4 (x_hi: 2, x_lo: 2; x = x_hi * 2 + x_lo), y: 4, z: 4, core: 2. Of those that a mesh axis runs over, the one named last changes fastest.
Arguments:
- plan: int32 [8192], P('shard'), may hold values from 0 to 1
- local_params: bfloat16 [2, 16, 8192, 2048], P(None, 'rep', 'shard'), may hold values from -6 to 6
- master: float32 [2, 8192, 2048], P(None, 'shard', 'rep'), may hold values from -6 to 6
- momentum: float32 [2, 8192, 2048], P(None, 'shard', 'rep'), may hold values from -6 to 6
- inner_weight: bfloat16 [16, 8192, 512], P('rep', 'shard'), may hold values from -0.0625 to 0.0625
- activations: bfloat16 [16, 2048, 8192], P('rep', 'shard'), may hold values from -6 to 6
- out_grad: bfloat16 [16, 2048, 512], P('rep', 'shard'), may hold values from -6 to 6
Outputs:
- new_params: bfloat16 [8192, 2048], P('shard')
- new_master: float32 [8192, 2048], P('shard', 'rep')
- new_momentum: float32 [8192, 2048], P('shard', 'rep')
- keys_out: bfloat16 [16, 2048, 512], P('rep', 'shard')
- input_grad: bfloat16 [16, 2048, 8192], P('rep', 'shard')
- weight_grad: bfloat16 [16, 8192, 512], P('rep', 'shard')
The draws below stay inside these ranges and needn't reach their ends.
All inputs are finite; a program needn't handle non-finite values.
Results may differ from the reference program's by a relative error of at most 0.017.
Values may be sent and summed in bfloat16 or wider, within the bound.
A program may use at most 128 MiB of HBM per device.

```python
import jax
import jax.numpy as jnp
from jax import lax

D = 8192
FRAGS = 2
TOK_DEV = 256
KVC = 2048
INNER = 512
TOKENS = 2048
N_REP = 16
N_SHARD = 8


def place_ends(drawn, stream_key, least, largest):
    longest = drawn.shape.index(max(drawn.shape))
    spots = []
    for shift in (0, 1):
        where = [jax.random.randint(jax.random.fold_in(stream_key, axis), (), 0, length) for axis, length in enumerate(drawn.shape)]
        where[longest] = (where[longest] + shift) % drawn.shape[longest]
        spots.append(tuple(where))
    return drawn.at[spots[0]].set(least).at[spots[1]].set(largest)


def block_levels(key, dims, cuts, smallest, high):
    gain = 1.0
    for axis_at, parts in cuts:
        draws = jax.random.uniform(jax.random.fold_in(jax.random.fold_in(key, 6), axis_at), (parts,), jnp.float32, smallest / len(cuts), high / len(cuts))
        gain = gain * jnp.repeat(jnp.exp(draws), dims[axis_at] // parts).reshape((-1,) + (1,) * (len(dims) - 1 - axis_at))
    return gain


def noise(key, extent, deviation, reach, split=(), held_as=jnp.bfloat16):
    entries = jax.random.normal(key, extent, jnp.float32) * deviation
    if len(split) > 0:
        entries = block_levels(key, extent, split, -0.22, 0.18) * entries
    return jnp.clip(entries, min=-reach, max=reach).astype(held_as)


def setup_inputs(seed: int = 0) -> dict:
    splits = jax.random.split(jax.random.key(seed), 8)
    plan = place_ends(jax.random.randint(splits[0], (D,), 0, FRAGS), jax.random.fold_in(splits[0], 1), 0, FRAGS - 1).astype(jnp.int32)
    local_params = noise(splits[1], (FRAGS, N_REP, D, KVC), 1.0, 6.0, ((1, 16), (2, 8)))
    master = noise(splits[2], (FRAGS, D, KVC), 1.0, 6.0, ((1, 8), (2, 16)), jnp.float32)
    momentum = noise(splits[3], (FRAGS, D, KVC), 1.0, 6.0, ((1, 8), (2, 16)), jnp.float32)
    inner_weight = noise(splits[4], (N_REP, D, INNER), D ** -0.5, 0.0625, ((0, 16), (1, 8)))
    activations = noise(splits[5], (N_REP, TOKENS, D), 1.0, 6.0, ((0, 16), (1, 8)))
    out_grad = noise(splits[6], (N_REP, TOKENS, INNER), 1.0, 6.0, ((0, 16), (1, 8)))
    return dict(plan=plan, local_params=local_params, master=master, momentum=momentum, inner_weight=inner_weight, activations=activations, out_grad=out_grad)


OUTER_LR = 0.7
OUTER_MU = 0.9


def replica_inner(operands):
    weight, inputs, cotangent = operands
    keys = jnp.dot(inputs, weight, preferred_element_type=jnp.float32).astype(jnp.bfloat16)
    back = lax.dot_general(cotangent, weight, (((1,), (1,)), ((), ())), preferred_element_type=jnp.float32).astype(jnp.bfloat16)
    groups_in = inputs.reshape(N_SHARD, TOK_DEV, D).astype(jnp.float32)
    groups_ct = cotangent.reshape(N_SHARD, TOK_DEV, INNER).astype(jnp.float32)
    terms = jnp.einsum("gtd,gtk->gdk", groups_in, groups_ct).astype(jnp.bfloat16)
    grad = jnp.sum(terms.astype(jnp.float32), axis=0).astype(jnp.bfloat16)
    return keys, back, grad


def reference(plan, local_params, master, momentum, inner_weight, activations, out_grad):
    local = local_params[0]
    master_now = master[0]
    moment_now = momentum[0]
    for fragment in range(1, FRAGS):
        picked = plan == fragment
        local = jnp.where(picked[None, :, None], local_params[fragment], local)
        master_now = jnp.where(picked[:, None], master[fragment], master_now)
        moment_now = jnp.where(picked[:, None], momentum[fragment], moment_now)
    total = jnp.sum(local.astype(jnp.float32), axis=0)
    outer_grad = master_now - total / N_REP
    new_momentum = OUTER_MU * moment_now + outer_grad
    new_master = master_now - OUTER_LR * (outer_grad + OUTER_MU * new_momentum)
    new_params = new_master.astype(jnp.bfloat16)
    keys_out, input_grad, weight_grad = lax.map(replica_inner, (inner_weight, activations, out_grad))
    return new_params, new_master, new_momentum, keys_out, input_grad, weight_grad
```

```python
import jax
import jax.numpy as jnp
from jax import lax
from jax.experimental import pallas as pl
from jax.experimental.pallas import tpu as pltpu
from jax.sharding import PartitionSpec as P

OUTER_LR = 0.7
OUTER_MU = 0.9
BF = jnp.bfloat16
F32 = jnp.float32
D, KVC, INNER, TOK = 8192, 2048, 512, 256
BLK = 1024
QR = 256
HALF = 512
QS = range(4)
HS = range(2)

KEYS = (
    [("g1", w, q) for w in "SUD" for q in QS]
    + [("g2", w, q) for w, qs in (("U", (0, 1)), ("D", (2, 3))) for q in qs]
    + [("g3", w, q) for w in "UD" for q in QS]
    + [("g4", q) for q in QS]
    + [("ra", w, q) for w in "UD" for q in QS]
    + [("x1", q) for q in QS]
    + [("rb", w, i) for w in "UD" for i in HS]
    + [("rc", w, q) for w in "UD" for q in QS]
    + [("x2", q) for q in QS]
    + [("c1", h) for h in HS]
    + [("zb", w) for w in "UD"]
    + [("zc", w, h) for w in "UD" for h in HS]
    + [("xr", h) for h in HS]
    + [("xp", h) for h in HS]
    + [("zp", w, h) for w in "UD" for h in HS]
    + [("zf", w) for w in "UD"]
    + [("c2", k, h) for k in range(4) for h in HS]
)
SEM = {key: i for i, key in enumerate(KEYS)}
LOCAL = (
    ["og", "plan", "w", "mast", "mom", "np", "nm", "nmo", "keys", "wg"]
    + [("act", j) for j in range(8)]
    + [("lp", k) for k in QS]
    + [("ig", j) for j in range(8)]
)
LSEM = {key: i for i, key in enumerate(LOCAL)}


def kernel(
    plan_h, lp_h, mast_h, mom_h, w_h, act_h, og_h,
    np_o, nm_o, nmo_o, keys_o, ig_o, wg_o,
    plan_v, pick, lpb, sel, cr, zb, zc, xr, npv, mast, mom, nm, nmo,
    act, og, wg, tt, ra, rx1, rb, rc, rx2, ig, acc, keysv,
    ss, rs, ls,
):
    rep, shard = lax.axis_index("rep"), lax.axis_index("shard")
    z, xl, c = rep // 4, (rep // 2) % 2, rep % 2
    y, xh = shard // 2, shard % 2
    yu, yd, yo = (y + 1) % 4, (y + 3) % 4, (y + 2) % 4
    zu, zd, zo = (z + 1) % 4, (z + 3) % 4, (z + 2) % 4
    me, sib = shard, y * 2 + 1 - xh
    bu, bd, bo = yu * 2 + xh, yd * 2 + xh, yo * 2 + xh
    bus, bds, bos = yu * 2 + 1 - xh, yd * 2 + 1 - xh, yo * 2 + 1 - xh
    to = {
        "U": (rep, bu), "D": (rep, bd), "S": (rep, sib),
        "X": (z * 4 + (1 - xl) * 2 + c, shard), "C": (z * 4 + xl * 2 + 1 - c, shard),
        "ZU": (zu * 4 + xl * 2 + c, shard), "ZD": (zd * 4 + xl * 2 + c, shard),
    }
    started = []

    def send(src, dst, key, way):
        copy = pltpu.make_async_remote_copy(
            src_ref=src, dst_ref=dst, send_sem=ss.at[SEM[key]], recv_sem=rs.at[SEM[key]],
            device_id=to[way], device_id_type=pl.DeviceIdType.MESH,
        )
        copy.start()
        started.append(copy)

    def arrived(dst, key, way):
        pltpu.make_async_remote_copy(
            src_ref=dst, dst_ref=dst, send_sem=ss.at[SEM[key]], recv_sem=rs.at[SEM[key]],
            device_id=to[way], device_id_type=pl.DeviceIdType.MESH,
        ).wait_recv()

    def fetch(src, dst, key):
        copy = pltpu.make_async_copy(src, dst, ls.at[LSEM[key]])
        copy.start()
        return copy

    def rows(block, q=0, n=QR):
        return pl.ds(pl.multiple_of(block * BLK + q * QR, QR), n)

    def cols(block, i=0, n=BLK):
        return pl.ds(pl.multiple_of(block * BLK + i, QR), n)

    f_og = fetch(og_h.at[0], og, "og")
    order = [bus, bds, bos, bu, bd, bo, sib, me]
    f_act = [fetch(act_h.at[0, :, cols(j)], act.at[:, cols(j)], ("act", i)) for i, j in enumerate(order)]
    f_plan = fetch(plan_h, plan_v, "plan")
    f_lp = [
        fetch(lp_h.at[:, 0, pl.ds(k * QR, QR)], lpb.at[k % 2], ("lp", k)) for k in (0, 1)
    ]
    f_w = fetch(w_h.at[0], wg.at[rows(me, 0, BLK)], "w")
    f_mast = fetch(mast_h, mast, "mast")
    f_mom = fetch(mom_h, mom, "mom")

    barrier = pltpu.get_barrier_semaphore()
    for device in to.values():
        pl.semaphore_signal(barrier, inc=1, device_id=device, device_id_type=pl.DeviceIdType.MESH)
    pl.semaphore_wait(barrier, len(to))

    for q in QS:
        for w in "SUD":
            send(w_h.at[0, pl.ds(q * QR, QR)], wg.at[rows(me, q)], ("g1", w, q), w)

    f_og.wait()

    def term(block):
        def sub(i, _):
            a = act[:, cols(block, i * QR, QR)]
            t = lax.dot_general(a, og[...], (((0,), (0,)), ((), ())), preferred_element_type=F32)
            tt[rows(block, i), :] = t.astype(BF)
            return 0

        lax.fori_loop(0, 4, sub, 0)

    for i, block in enumerate(order):
        f_act[i].wait()
        term(block)
        if i == 0:
            for q in QS:
                send(tt.at[rows(block, q)], ra.at[0, pl.ds(q * QR, QR)], ("ra", "U", q), "U")
        if i == 1:
            for q in QS:
                send(tt.at[rows(block, q)], ra.at[1, pl.ds(q * QR, QR)], ("ra", "D", q), "D")
        if i == 2:
            for q in QS:
                send(tt.at[rows(block, q)], rx1.at[pl.ds(q * QR, QR)], ("x1", q), "S")
        if i == 3:
            for q in (0, 1):
                send(tt.at[rows(block, q)], rc.at[0, pl.ds(q * QR, QR)], ("rc", "U", q), "U")
        if i == 4:
            for q in (2, 3):
                send(tt.at[rows(block, q)], rc.at[1, pl.ds(q * QR, QR)], ("rc", "D", q), "D")

    f_plan.wait()
    for g in range(8):
        line = plan_v[pl.ds(g, 1), :].astype(F32)
        pick[pl.ds(g * 128, 128), :] = jnp.broadcast_to(line, (128, 128)).T

    for k in QS:
        f_lp[k].wait()

        def choose(i, _, k=k):
            r = pl.multiple_of(i * 64, 64)
            mask = pick[pl.ds(k * QR + r, 64), :] == 1.0
            for b in range(16):
                a0 = lpb[k % 2, 0, pl.ds(r, 64), b * 128 : (b + 1) * 128].astype(F32)
                a1 = lpb[k % 2, 1, pl.ds(r, 64), b * 128 : (b + 1) * 128].astype(F32)
                sel[b % 2, k // 2, b // 4, (b // 2) % 2, pl.ds((k % 2) * QR + r, 64), :] = jnp.where(
                    mask, a1, a0
                ).astype(BF)
            return 0

        lax.fori_loop(0, 4, choose, 0)
        if k < 2:
            f_lp.append(
                fetch(lp_h.at[:, 0, pl.ds((k + 2) * QR, QR)], lpb.at[k % 2], ("lp", k + 2))
            )
        if k % 2 == 1:
            send(sel.at[1 - c, k // 2], cr.at[k // 2], ("c1", k // 2), "C")

    acc[...] = jnp.zeros_like(acc)
    out_copies = []

    def layer(block, n):
        def sub(i, _):
            at = cols(block, i * HALF, HALF)
            w = wg[at, :]
            acc[...] += jnp.dot(act[:, at], w, preferred_element_type=F32)
            ig[:, at] = lax.dot_general(
                og[...], w, (((1,), (1,)), ((), ())), preferred_element_type=F32
            ).astype(BF)
            return 0

        lax.fori_loop(0, 2, sub, 0)
        out_copies.append(fetch(ig.at[:, cols(block)], ig_o.at[0, :, cols(block)], ("ig", n)))

    def add_into(dst, dst_row, *sources):
        def sub(i, _):
            at = pl.ds(pl.multiple_of(dst_row + i * 64, 64), 64)
            total = dst[at, :].astype(F32)
            for ref, row in sources:
                total = total + ref[pl.ds(row + i * 64, 64), :].astype(F32)
            dst[at, :] = total.astype(BF)
            return 0

        lax.fori_loop(0, QR // 64, sub, 0)

    f_w.wait()
    layer(me, 0)

    def core_sum(zz, h):
        def sub(i, _):
            at = pl.ds(pl.multiple_of(i * 128, 128), 128)
            for l in HS:
                sel[c, h, zz, l, at, :] = (
                    sel[c, h, zz, l, at, :].astype(F32) + cr[h, zz, l, at, :].astype(F32)
                ).astype(BF)
            return 0

        lax.fori_loop(0, 4, sub, 0)

    for h in HS:
        arrived(cr.at[h], ("c1", h), "C")
    core_sum(zo, 0)
    send(sel.at[c, 0, zo], zb.at[1], ("zb", "D"), "ZD")
    core_sum(zo, 1)
    send(sel.at[c, 1, zo], zb.at[0], ("zb", "U"), "ZU")
    core_sum(zu, 0)
    send(sel.at[c, 0, zu], zc.at[0, 0], ("zc", "U", 0), "ZU")
    core_sum(zd, 1)
    send(sel.at[c, 1, zd], zc.at[1, 1], ("zc", "D", 1), "ZD")
    core_sum(zu, 1)
    core_sum(zd, 0)
    core_sum(z, 0)
    core_sum(z, 1)

    for q in (0, 1):
        arrived(wg.at[rows(bd, q)], ("g1", "U", q), "D")
        send(wg.at[rows(bd, q)], wg.at[rows(bd, q)], ("g2", "U", q), "U")
        arrived(wg.at[rows(bu, q)], ("g1", "D", q), "U")
    for q in (2, 3):
        arrived(wg.at[rows(bu, q)], ("g1", "D", q), "U")
        send(wg.at[rows(bu, q)], wg.at[rows(bu, q)], ("g2", "D", q), "D")
        arrived(wg.at[rows(bd, q)], ("g1", "U", q), "D")

    def z_add(dst, h, zz, way):
        def sub(i, _):
            at = pl.ds(pl.multiple_of(i * 128, 128), 128)
            for l in HS:
                sel[c, h, zz, l, at, :] = (
                    sel[c, h, zz, l, at, :].astype(F32) + zb[way, l, at, :].astype(F32)
                ).astype(BF)
            return 0

        lax.fori_loop(0, 4, sub, 0)

    arrived(zb.at[0], ("zb", "U"), "ZD")
    z_add(sel, 1, zu, 0)
    send(sel.at[c, 1, zu], zc.at[0, 1], ("zc", "U", 1), "ZU")
    arrived(zb.at[1], ("zb", "D"), "ZU")
    z_add(sel, 0, zd, 1)
    send(sel.at[c, 0, zd], zc.at[1, 0], ("zc", "D", 0), "ZD")

    layer(bd, 1)
    layer(bu, 2)
    for q in QS:
        arrived(wg.at[rows(sib, q)], ("g1", "S", q), "S")
    layer(sib, 3)

    for h in HS:
        arrived(zc.at[0, h], ("zc", "U", h), "ZD")
        arrived(zc.at[1, h], ("zc", "D", h), "ZU")

        def z_sum(i, _, h=h):
            at = pl.ds(pl.multiple_of(i * 128, 128), 128)
            sel[c, h, z, 1 - xl, at, :] = (
                sel[c, h, z, 1 - xl, at, :].astype(F32)
                + zc[0, h, 1 - xl, at, :].astype(F32)
                + zc[1, h, 1 - xl, at, :].astype(F32)
            ).astype(BF)
            return 0

        lax.fori_loop(0, 4, z_sum, 0)
        send(sel.at[c, h, z, 1 - xl], xr.at[h], ("xr", h), "X")

    for q in (0, 2, 1, 3):
        arrived(rx1.at[pl.ds(q * QR, QR)], ("x1", q), "S")
        add_into(tt, bo * BLK + q * QR, (rx1, q * QR))
        way = "D" if q < 2 else "U"
        side = 1 if q < 2 else 0
        send(tt.at[rows(bo, q)], rb.at[side, pl.ds((q % 2) * QR, QR)], ("rb", way, q % 2), way)

    for q in (0, 1):
        for w in "UD":
            send(wg.at[rows(sib, q)], wg.at[rows(sib, q)], ("g3", w, q), w)

    for q in QS:
        arrived(ra.at[0, pl.ds(q * QR, QR)], ("ra", "U", q), "D")
        arrived(ra.at[1, pl.ds(q * QR, QR)], ("ra", "D", q), "U")
        add_into(tt, sib * BLK + q * QR, (ra.at[0], q * QR), (ra.at[1], q * QR))
        send(tt.at[rows(sib, q)], rx2.at[pl.ds(q * QR, QR)], ("x2", q), "S")

    f_mast.wait()
    f_mom.wait()
    for h in HS:
        arrived(xr.at[h], ("xr", h), "X")

        def update(i, _, h=h):
            at = pl.ds(pl.multiple_of(i * 64, 64), 64)
            to_row = pl.ds(pl.multiple_of(h * HALF + i * 64, 64), 64)
            total = (
                sel[c, h, z, xl, at, :].astype(F32)
                + zc[0, h, xl, at, :].astype(F32)
                + zc[1, h, xl, at, :].astype(F32)
                + xr[h, at, :].astype(F32)
            )
            mask = pick[to_row, :] == 1.0
            master_now = jnp.where(mask, mast[1, to_row, :], mast[0, to_row, :])
            moment_now = jnp.where(mask, mom[1, to_row, :], mom[0, to_row, :])
            outer_grad = master_now - total / 16
            new_momentum = OUTER_MU * moment_now + outer_grad
            new_master = master_now - OUTER_LR * (outer_grad + OUTER_MU * new_momentum)
            nmo[to_row, :] = new_momentum
            nm[to_row, :] = new_master
            npv[c, h, z, xl, at, :] = new_master.astype(BF)
            return 0

        lax.fori_loop(0, 8, update, 0)
        send(npv.at[c, h, z, xl], npv.at[c, h, z, xl], ("xp", h), "X")
    out_copies.append(fetch(nm, nm_o, "nm"))
    out_copies.append(fetch(nmo, nmo_o, "nmo"))

    for q in QS:
        way, back = ("U", "D") if q < 2 else ("D", "U")
        arrived(wg.at[rows(bo, q)], ("g2", way, q), back)
        send(wg.at[rows(bo, q)], wg.at[rows(bo, q)], ("g4", q), "S")

    for h in HS:
        arrived(npv.at[c, h, z, 1 - xl], ("xp", h), "X")
        for w in "UD":
            send(npv.at[c, h, z], npv.at[c, h, z], ("zp", w, h), "Z" + w)
        send(npv.at[c, h, z], npv.at[c, h, z], ("c2", 0, h), "C")

    layer(bo, 4)

    for i in HS:
        arrived(rb.at[0, pl.ds(i * QR, QR)], ("rb", "U", i), "D")
        add_into(tt, bu * BLK + (2 + i) * QR, (rb.at[0], i * QR))
        q = 2 + i
        send(tt.at[rows(bu, q)], rc.at[0, pl.ds(q * QR, QR)], ("rc", "U", q), "U")
        arrived(rb.at[1, pl.ds(i * QR, QR)], ("rb", "D", i), "U")
        add_into(tt, bd * BLK + i * QR, (rb.at[1], i * QR))
        send(tt.at[rows(bd, i)], rc.at[1, pl.ds(i * QR, QR)], ("rc", "D", i), "D")

    for q in (2, 3):
        for w in "UD":
            send(wg.at[rows(sib, q)], wg.at[rows(sib, q)], ("g3", w, q), w)

    for h in HS:
        arrived(npv.at[c, h, zd], ("zp", "U", h), "ZD")
        if h == 0:
            send(npv.at[c, 0, zd], npv.at[c, 0, zd], ("zf", "U"), "ZU")
        send(npv.at[c, h, zd], npv.at[c, h, zd], ("c2", 1, h), "C")
        arrived(npv.at[c, h, zu], ("zp", "D", h), "ZU")
        if h == 1:
            send(npv.at[c, 1, zu], npv.at[c, 1, zu], ("zf", "D"), "ZD")
        send(npv.at[c, h, zu], npv.at[c, h, zu], ("c2", 2, h), "C")
    arrived(npv.at[c, 0, zo], ("zf", "U"), "ZD")
    send(npv.at[c, 0, zo], npv.at[c, 0, zo], ("c2", 3, 0), "C")
    arrived(npv.at[c, 1, zo], ("zf", "D"), "ZU")
    send(npv.at[c, 1, zo], npv.at[c, 1, zo], ("c2", 3, 1), "C")

    for h in HS:
        for k, zz in enumerate((z, zd, zu, zo)):
            arrived(npv.at[1 - c, h, zz], ("c2", k, h), "C")
    for b in range(16):
        for h in HS:
            pltpu.make_async_copy(
                npv.at[b % 2, h, b // 4, (b // 2) % 2],
                np_o.at[pl.ds(h * HALF, HALF), pl.ds(b * 128, 128)],
                ls.at[LSEM["np"]],
            ).start()

    for q in QS:
        arrived(wg.at[rows(bos, q)], ("g4", q), "S")
    layer(bos, 5)

    for q in QS:
        arrived(rx2.at[pl.ds(q * QR, QR)], ("x2", q), "S")
    for q in QS:
        arrived(rc.at[0, pl.ds(q * QR, QR)], ("rc", "U", q), "D")
        arrived(rc.at[1, pl.ds(q * QR, QR)], ("rc", "D", q), "U")
        add_into(tt, me * BLK + q * QR, (rc.at[0], q * QR), (rc.at[1], q * QR), (rx2, q * QR))
    out_copies.append(fetch(tt.at[rows(me, 0, BLK)], wg_o.at[0], "wg"))

    for n, (block, way, back) in enumerate(((bds, "U", "D"), (bus, "D", "U"))):
        for q in QS:
            arrived(wg.at[rows(block, q)], ("g3", way, q), back)
        layer(block, 6 + n)
    keysv[...] = acc[...].astype(BF)
    out_copies.append(fetch(keysv, keys_o.at[0], "keys"))

    for copy in started:
        copy.wait_send()
    for copy in out_copies:
        copy.wait()
    pltpu.make_async_copy(np_o, np_o, ls.at[LSEM["np"]]).wait()


def body(plan, local_params, master, momentum, inner_weight, activations, out_grad):
    vm = pltpu.VMEM
    any_spec = pl.BlockSpec(memory_space=pl.ANY)
    return pl.pallas_call(
        kernel,
        out_shape=(
            jax.ShapeDtypeStruct((BLK, KVC), BF),
            jax.ShapeDtypeStruct((BLK, 128), F32),
            jax.ShapeDtypeStruct((BLK, 128), F32),
            jax.ShapeDtypeStruct((1, TOK, INNER), BF),
            jax.ShapeDtypeStruct((1, TOK, D), BF),
            jax.ShapeDtypeStruct((1, BLK, INNER), BF),
        ),
        in_specs=[any_spec] * 7,
        out_specs=[any_spec] * 6,
        scratch_shapes=[
            vm((8, 128), jnp.int32),
            vm((BLK, 128), F32),
            vm((2, 2, QR, KVC), BF),
            vm((2, 2, 4, 2, HALF, 128), BF),
            vm((2, 4, 2, HALF, 128), BF),
            vm((2, 2, HALF, 128), BF),
            vm((2, 2, 2, HALF, 128), BF),
            vm((2, HALF, 128), BF),
            vm((2, 2, 4, 2, HALF, 128), BF),
            vm((2, BLK, 128), F32),
            vm((2, BLK, 128), F32),
            vm((BLK, 128), F32),
            vm((BLK, 128), F32),
            vm((TOK, D), BF),
            vm((TOK, INNER), BF),
            vm((D, INNER), BF),
            vm((D, INNER), BF),
            vm((2, BLK, INNER), BF),
            vm((BLK, INNER), BF),
            vm((2, HALF, INNER), BF),
            vm((2, BLK, INNER), BF),
            vm((BLK, INNER), BF),
            vm((TOK, D), BF),
            vm((TOK, INNER), F32),
            vm((TOK, INNER), BF),
            pltpu.SemaphoreType.DMA((len(KEYS),)),
            pltpu.SemaphoreType.DMA((len(KEYS),)),
            pltpu.SemaphoreType.DMA((len(LOCAL),)),
        ],
        compiler_params=pltpu.CompilerParams(
            collective_id=0, has_side_effects=True, vmem_limit_bytes=60 << 20
        ),
        cost_estimate=pl.CostEstimate(
            flops=6 * TOK * D * INNER, bytes_accessed=26 << 20, transcendentals=0
        ),
        name="sync_and_layer",
    )(plan.reshape(8, 128), local_params, master, momentum, inner_weight, activations, out_grad)


def solution(mesh):
    placed = (
        P("shard"),
        P(None, "rep", "shard", None),
        P(None, "shard", "rep"),
        P(None, "shard", "rep"),
        P("rep", "shard", None),
        P("rep", "shard", None),
        P("rep", "shard", None),
    )
    return jax.shard_map(
        body,
        mesh=mesh,
        in_specs=placed,
        out_specs=(
            P("shard", None),
            P("shard", "rep"),
            P("shard", "rep"),
            P("rep", "shard", None),
            P("rep", "shard", None),
            P("rep", "shard", None),
        ),
        check_vma=False,
    )
```

```python
import jax
import jax.numpy as jnp
from jax import lax
from jax.experimental import pallas as pl
from jax.experimental.pallas import tpu as pltpu
from jax.sharding import PartitionSpec as P

OUTER_LR = 0.7
OUTER_MU = 0.9
BF = jnp.bfloat16
F32 = jnp.float32
D, KVC, INNER, TOK = 8192, 2048, 512, 256
BLK = 1024
QR = 256
HALF = 512
QS = range(4)
HS = range(2)

KEYS = (
    [("og",)]
    + [("ax", k) for k in range(4)]
    + [("g1", w, q) for w in "SUD" for q in QS]
    + [("g2", w, q) for w, qs in (("U", (0, 1)), ("D", (2, 3))) for q in qs]
    + [("g3", w, q) for w in "UD" for q in QS]
    + [("g4", q) for q in (1, 2)]
    + [("g5", w) for w in "UD"]
    + [("rb", w, i) for w in "UD" for i in HS]
    + [("rc", w, q) for w in "UD" for q in QS]
    + [("c1", h) for h in HS]
    + [("zb", w) for w in "UD"]
    + [("zc", w, h) for w in "UD" for h in HS]
    + [("xr", h) for h in HS]
    + [("xp", h) for h in HS]
    + [("zp", w, h) for w in "UD" for h in HS]
    + [("zf", w) for w in "UD"]
    + [("c2", k, h) for k in range(4) for h in HS]
)
SEM = {key: i for i, key in enumerate(KEYS)}
LOCAL = (
    ["og", "plan", "w", "mast", "mom", "np"]
    + [("act", j) for j in range(8)]
    + [("lp", k) for k in QS]
)
LSEM = {key: i for i, key in enumerate(LOCAL)}


def kernel(
    plan_h, lp_h, mast_h, mom_h, w_h, act_h, og_h,
    np_o, nm, nmo, keys_o, ig, wg_o,
    plan_v, pick, lpb, sel, cr, zb, zc, xr, npv, mast, mom,
    act, og, acts, ogs, wg, tt, rb, rc, acc,
    ss, rs, ls,
):
    rep, shard = lax.axis_index("rep"), lax.axis_index("shard")
    z, xl, c = rep // 4, (rep // 2) % 2, rep % 2
    y, xh = shard // 2, shard % 2
    yu, yd, yo = (y + 1) % 4, (y + 3) % 4, (y + 2) % 4
    zu, zd, zo = (z + 1) % 4, (z + 3) % 4, (z + 2) % 4
    me, sib = shard, y * 2 + 1 - xh
    bu, bd, bo = yu * 2 + xh, yd * 2 + xh, yo * 2 + xh
    bus, bds, bos = yu * 2 + 1 - xh, yd * 2 + 1 - xh, yo * 2 + 1 - xh
    to = {
        "U": (rep, bu), "D": (rep, bd), "S": (rep, sib),
        "X": (z * 4 + (1 - xl) * 2 + c, shard), "C": (z * 4 + xl * 2 + 1 - c, shard),
        "ZU": (zu * 4 + xl * 2 + c, shard), "ZD": (zd * 4 + xl * 2 + c, shard),
    }
    started = []

    def send(src, dst, key, way):
        copy = pltpu.make_async_remote_copy(
            src_ref=src, dst_ref=dst, send_sem=ss.at[SEM[key]], recv_sem=rs.at[SEM[key]],
            device_id=to[way], device_id_type=pl.DeviceIdType.MESH,
        )
        copy.start()
        started.append(copy)

    def arrived(dst, key, way):
        pltpu.make_async_remote_copy(
            src_ref=dst, dst_ref=dst, send_sem=ss.at[SEM[key]], recv_sem=rs.at[SEM[key]],
            device_id=to[way], device_id_type=pl.DeviceIdType.MESH,
        ).wait_recv()

    def fetch(src, dst, key):
        copy = pltpu.make_async_copy(src, dst, ls.at[LSEM[key]])
        copy.start()
        return copy

    def rows(block, q=0, n=QR):
        return pl.ds(pl.multiple_of(block * BLK + q * QR, QR), n)

    def cols(block, i=0, n=BLK):
        return pl.ds(pl.multiple_of(block * BLK + i, QR), n)

    f_plan = fetch(plan_h, plan_v, "plan")
    f_lp = [
        fetch(lp_h.at[:, 0, pl.ds(k * QR, QR)], lpb.at[k % 2], ("lp", k)) for k in (0, 1)
    ]
    f_og = fetch(og_h.at[0], og, "og")
    f_w = fetch(w_h.at[0], wg.at[rows(me, 0, BLK)], "w")
    order = [me, bo, bu, bd, bus, bds, bos, sib]
    f_act = [fetch(act_h.at[0, :, cols(j)], act.at[:, cols(j)], ("act", i)) for i, j in enumerate(order)]
    f_mast = fetch(mast_h, mast, "mast")
    f_mom = fetch(mom_h, mom, "mom")

    barrier = pltpu.get_barrier_semaphore()
    for device in to.values():
        pl.semaphore_signal(barrier, inc=1, device_id=device, device_id_type=pl.DeviceIdType.MESH)
    pl.semaphore_wait(barrier, len(to))

    def tokens_to_sibling(k):
        yy = (yo, yu, yd, y)[k]
        send(act_h.at[0, :, cols(yy * 2 + 1 - xh)], acts.at[yy], ("ax", k), "S")

    for q in QS:
        for w in "UD":
            send(w_h.at[0, pl.ds(q * QR, QR)], wg.at[rows(me, q)], ("g1", w, q), w)
        if q == 0:
            send(og_h.at[0], ogs, ("og",), "S")
            tokens_to_sibling(0)
    tokens_to_sibling(1)

    def weight_to_sibling(q):
        send(w_h.at[0, pl.ds(q * QR, QR)], wg.at[rows(me, q)], ("g1", "S", q), "S")

    f_plan.wait()
    for g in range(8):
        line = plan_v[pl.ds(g, 1), :].astype(F32)
        pick[pl.ds(g * 128, 128), :] = jnp.broadcast_to(line, (128, 128)).T

    for k in QS:
        f_lp[k].wait()

        def choose(i, _, k=k):
            r = pl.multiple_of(i * 64, 64)
            mask = pick[pl.ds(k * QR + r, 64), :] == 1.0
            for b in range(16):
                a0 = lpb[k % 2, 0, pl.ds(r, 64), b * 128 : (b + 1) * 128].astype(F32)
                a1 = lpb[k % 2, 1, pl.ds(r, 64), b * 128 : (b + 1) * 128].astype(F32)
                sel[b % 2, k // 2, b // 4, (b // 2) % 2, pl.ds((k % 2) * QR + r, 64), :] = jnp.where(
                    mask, a1, a0
                ).astype(BF)
            return 0

        lax.fori_loop(0, 4, choose, 0)
        if k < 2:
            f_lp.append(
                fetch(lp_h.at[:, 0, pl.ds((k + 2) * QR, QR)], lpb.at[k % 2], ("lp", k + 2))
            )
        if k % 2 == 1:
            send(sel.at[1 - c, k // 2], cr.at[k // 2], ("c1", k // 2), "C")

    f_og.wait()
    acc[...] = jnp.zeros_like(acc)

    def layer(block, q0=0, n=4):
        def sub(i, _):
            at = cols(block, (q0 + i) * QR, QR)
            w = wg[at, :]
            acc[...] += jnp.dot(act[:, at], w, preferred_element_type=F32)
            ig[0, :, at] = lax.dot_general(
                og[...], w, (((1,), (1,)), ((), ())), preferred_element_type=F32
            ).astype(BF)
            return 0

        lax.fori_loop(0, n, sub, 0)

    def term(k):
        yy = (yo, yu, yd, y)[k]
        arrived(acts.at[yy], ("ax", k), "S")
        if k == 0:
            tokens_to_sibling(2)

        def sub(i, _):
            at = pl.ds(pl.multiple_of(i * QR, QR), QR)
            over_tokens = (((0,), (0,)), ((), ()))
            t = lax.dot_general(
                act[:, cols(yy * 2 + xh, i * QR, QR)], og[...], over_tokens, preferred_element_type=F32
            ) + lax.dot_general(acts[yy, :, at], ogs[...], over_tokens, preferred_element_type=F32)
            tt[rows(yy, i), :] = t.astype(BF)
            return 0

        lax.fori_loop(0, 4, sub, 0)

    def add_into(dst, dst_row, *sources):
        def sub(i, _):
            at = pl.ds(pl.multiple_of(dst_row + i * 64, 64), 64)
            total = dst[at, :].astype(F32)
            for ref, row in sources:
                total = total + ref[pl.ds(row + i * 64, 64), :].astype(F32)
            dst[at, :] = total.astype(BF)
            return 0

        lax.fori_loop(0, QR // 64, sub, 0)

    f_w.wait()
    for copy in f_act:
        copy.wait()
    layer(me)

    def core_sum(zz, h):
        def sub(i, _):
            at = pl.ds(pl.multiple_of(i * 128, 128), 128)
            for l in HS:
                sel[c, h, zz, l, at, :] = (
                    sel[c, h, zz, l, at, :].astype(F32) + cr[h, zz, l, at, :].astype(F32)
                ).astype(BF)
            return 0

        lax.fori_loop(0, 4, sub, 0)

    for h in HS:
        arrived(cr.at[h], ("c1", h), "C")
    core_sum(zo, 0)
    send(sel.at[c, 0, zo], zb.at[1], ("zb", "D"), "ZD")
    core_sum(zo, 1)
    send(sel.at[c, 1, zo], zb.at[0], ("zb", "U"), "ZU")
    core_sum(zu, 0)
    send(sel.at[c, 0, zu], zc.at[0, 0], ("zc", "U", 0), "ZU")
    core_sum(zd, 1)
    send(sel.at[c, 1, zd], zc.at[1, 1], ("zc", "D", 1), "ZD")
    core_sum(zu, 1)
    core_sum(zd, 0)
    core_sum(z, 0)
    core_sum(z, 1)

    arrived(ogs, ("og",), "S")
    term(0)
    for q in (0, 2, 1, 3):
        way = "D" if q < 2 else "U"
        side = 1 if q < 2 else 0
        send(tt.at[rows(yo, q)], rb.at[side, pl.ds((q % 2) * QR, QR)], ("rb", way, q % 2), way)

    for q in (0, 1):
        arrived(wg.at[rows(bd, q)], ("g1", "U", q), "D")
        send(wg.at[rows(bd, q)], wg.at[rows(bd, q)], ("g2", "U", q), "U")
        arrived(wg.at[rows(bu, q)], ("g1", "D", q), "U")
    for q in (2, 3):
        arrived(wg.at[rows(bu, q)], ("g1", "D", q), "U")
        send(wg.at[rows(bu, q)], wg.at[rows(bu, q)], ("g2", "D", q), "D")
        arrived(wg.at[rows(bd, q)], ("g1", "U", q), "D")

    def z_add(h, zz, way):
        def sub(i, _):
            at = pl.ds(pl.multiple_of(i * 128, 128), 128)
            for l in HS:
                sel[c, h, zz, l, at, :] = (
                    sel[c, h, zz, l, at, :].astype(F32) + zb[way, l, at, :].astype(F32)
                ).astype(BF)
            return 0

        lax.fori_loop(0, 4, sub, 0)

    arrived(zb.at[0], ("zb", "U"), "ZD")
    z_add(1, zu, 0)
    send(sel.at[c, 1, zu], zc.at[0, 1], ("zc", "U", 1), "ZU")
    arrived(zb.at[1], ("zb", "D"), "ZU")
    z_add(0, zd, 1)
    send(sel.at[c, 0, zd], zc.at[1, 0], ("zc", "D", 0), "ZD")

    term(1)
    for q in (0, 1):
        send(tt.at[rows(yu, q)], rc.at[0, pl.ds(q * QR, QR)], ("rc", "U", q), "U")

    for h in HS:
        arrived(zc.at[0, h], ("zc", "U", h), "ZD")
        arrived(zc.at[1, h], ("zc", "D", h), "ZU")

        def z_sum(i, _, h=h):
            at = pl.ds(pl.multiple_of(i * 128, 128), 128)
            sel[c, h, z, 1 - xl, at, :] = (
                sel[c, h, z, 1 - xl, at, :].astype(F32)
                + zc[0, h, 1 - xl, at, :].astype(F32)
                + zc[1, h, 1 - xl, at, :].astype(F32)
            ).astype(BF)
            return 0

        lax.fori_loop(0, 4, z_sum, 0)
        send(sel.at[c, h, z, 1 - xl], xr.at[h], ("xr", h), "X")

    weight_to_sibling(0)
    layer(bd)
    layer(bu)

    term(2)
    for q in (2, 3):
        send(tt.at[rows(yd, q)], rc.at[1, pl.ds(q * QR, QR)], ("rc", "D", q), "D")

    for i in HS:
        q = 2 + i
        arrived(rb.at[0, pl.ds(i * QR, QR)], ("rb", "U", i), "D")
        add_into(tt, yu * BLK + q * QR, (rb.at[0], i * QR))
        send(tt.at[rows(yu, q)], rc.at[0, pl.ds(q * QR, QR)], ("rc", "U", q), "U")
        arrived(rb.at[1, pl.ds(i * QR, QR)], ("rb", "D", i), "U")
        add_into(tt, yd * BLK + i * QR, (rb.at[1], i * QR))
        send(tt.at[rows(yd, i)], rc.at[1, pl.ds(i * QR, QR)], ("rc", "D", i), "D")

    f_mast.wait()
    f_mom.wait()
    for h in HS:
        arrived(xr.at[h], ("xr", h), "X")

        def update(i, _, h=h):
            at = pl.ds(pl.multiple_of(i * 64, 64), 64)
            to_row = pl.ds(pl.multiple_of(h * HALF + i * 64, 64), 64)
            total = (
                sel[c, h, z, xl, at, :].astype(F32)
                + zc[0, h, xl, at, :].astype(F32)
                + zc[1, h, xl, at, :].astype(F32)
                + xr[h, at, :].astype(F32)
            )
            mask = pick[to_row, :] == 1.0
            master_now = jnp.where(mask, mast[1, to_row, :], mast[0, to_row, :])
            moment_now = jnp.where(mask, mom[1, to_row, :], mom[0, to_row, :])
            outer_grad = master_now - total / 16
            new_momentum = OUTER_MU * moment_now + outer_grad
            new_master = master_now - OUTER_LR * (outer_grad + OUTER_MU * new_momentum)
            nmo[to_row, :] = new_momentum
            nm[to_row, :] = new_master
            npv[c, h, z, xl, at, :] = new_master.astype(BF)
            return 0

        lax.fori_loop(0, 8, update, 0)
        send(npv.at[c, h, z, xl], npv.at[c, h, z, xl], ("xp", h), "X")

    for q in (3, 1, 2):
        weight_to_sibling(q)
    tokens_to_sibling(3)

    for q in QS:
        way, back = ("U", "D") if q < 2 else ("D", "U")
        arrived(wg.at[rows(bo, q)], ("g2", way, q), back)
        if q in (1, 2):
            send(wg.at[rows(bo, q)], wg.at[rows(bo, q)], ("g4", q), "S")
    layer(bo)

    def pass_on(q):
        arrived(wg.at[rows(sib, q)], ("g1", "S", q), "S")
        for w in "UD":
            send(wg.at[rows(sib, q)], wg.at[rows(sib, q)], ("g3", w, q), w)

    pass_on(0)

    for h in HS:
        arrived(npv.at[c, h, z, 1 - xl], ("xp", h), "X")
        for w in "UD":
            send(npv.at[c, h, z], npv.at[c, h, z], ("zp", w, h), "Z" + w)
        send(npv.at[c, h, z], npv.at[c, h, z], ("c2", 0, h), "C")

    for h in HS:
        pass_on((3, 1)[h])
        arrived(npv.at[c, h, zd], ("zp", "U", h), "ZD")
        if h == 0:
            send(npv.at[c, 0, zd], npv.at[c, 0, zd], ("zf", "U"), "ZU")
        send(npv.at[c, h, zd], npv.at[c, h, zd], ("c2", 1, h), "C")
        arrived(npv.at[c, h, zu], ("zp", "D", h), "ZU")
        if h == 1:
            send(npv.at[c, 1, zu], npv.at[c, 1, zu], ("zf", "D"), "ZD")
        send(npv.at[c, h, zu], npv.at[c, h, zu], ("c2", 2, h), "C")
    pass_on(2)

    arrived(wg.at[rows(bds, 0)], ("g3", "U", 0), "D")
    send(wg.at[rows(bds, 0)], wg.at[rows(bds, 0)], ("g5", "U"), "U")
    arrived(wg.at[rows(bus, 3)], ("g3", "D", 3), "U")
    send(wg.at[rows(bus, 3)], wg.at[rows(bus, 3)], ("g5", "D"), "D")

    arrived(npv.at[c, 0, zo], ("zf", "U"), "ZD")
    send(npv.at[c, 0, zo], npv.at[c, 0, zo], ("c2", 3, 0), "C")
    arrived(npv.at[c, 1, zo], ("zf", "D"), "ZU")
    send(npv.at[c, 1, zo], npv.at[c, 1, zo], ("c2", 3, 1), "C")

    layer(sib)

    term(3)
    for q in QS:
        arrived(rc.at[0, pl.ds(q * QR, QR)], ("rc", "U", q), "D")
        arrived(rc.at[1, pl.ds(q * QR, QR)], ("rc", "D", q), "U")

        def grad_sum(i, _, q=q):
            at = pl.ds(pl.multiple_of(q * QR + i * 64, 64), 64)
            wg_o[0, at, :] = (
                tt[pl.ds(pl.multiple_of(y * BLK + q * QR + i * 64, 64), 64), :].astype(F32)
                + rc[0, at, :].astype(F32)
                + rc[1, at, :].astype(F32)
            ).astype(BF)
            return 0

        lax.fori_loop(0, 4, grad_sum, 0)

    for h in HS:
        for k, zz in enumerate((z, zd, zu, zo)):
            arrived(npv.at[1 - c, h, zz], ("c2", k, h), "C")
    for b in range(16):
        for h in HS:
            pltpu.make_async_copy(
                npv.at[b % 2, h, b // 4, (b // 2) % 2],
                np_o.at[pl.ds(h * HALF, HALF), pl.ds(b * 128, 128)],
                ls.at[LSEM["np"]],
            ).start()

    layer(bds, 0, 1)
    layer(bus, 3, 1)
    arrived(wg.at[rows(bds, 3)], ("g3", "U", 3), "D")
    layer(bds, 3, 1)
    arrived(wg.at[rows(bus, 0)], ("g3", "D", 0), "U")
    layer(bus, 0, 1)
    for q in (1, 2):
        arrived(wg.at[rows(bos, q)], ("g4", q), "S")
        arrived(wg.at[rows(bds, q)], ("g3", "U", q), "D")
        arrived(wg.at[rows(bus, q)], ("g3", "D", q), "U")
        for block in (bos, bds, bus):
            layer(block, q, 1)
    arrived(wg.at[rows(bos, 0)], ("g5", "U"), "D")
    layer(bos, 0, 1)
    arrived(wg.at[rows(bos, 3)], ("g5", "D"), "U")
    layer(bos, 3, 1)
    keys_o[0] = acc[...].astype(BF)

    for copy in started:
        copy.wait_send()
    pltpu.make_async_copy(np_o, np_o, ls.at[LSEM["np"]]).wait()


def write_out(*refs):
    n = len(refs) // 2
    sems = refs[-1]
    copies = [pltpu.make_async_copy(refs[i], refs[n + i], sems.at[i]) for i in range(n)]
    for copy in copies:
        copy.start()
    for copy in copies:
        copy.wait()


def body(plan, local_params, master, momentum, inner_weight, activations, out_grad):
    vm = pltpu.VMEM
    any_spec = pl.BlockSpec(memory_space=pl.ANY)
    vm_spec = pl.BlockSpec(memory_space=vm)
    outs = (
        ((BLK, KVC), BF),
        ((BLK, 128), F32),
        ((BLK, 128), F32),
        ((1, TOK, INNER), BF),
        ((1, TOK, D), BF),
        ((1, BLK, INNER), BF),
    )
    given = (plan.reshape(8, 128), local_params, master, momentum, inner_weight, activations, out_grad)
    results = pl.pallas_call(
        kernel,
        out_shape=tuple(vm(*out) for out in outs),
        in_specs=[any_spec] * 7,
        out_specs=[vm_spec] * 6,
        scratch_shapes=[
            vm((8, 128), jnp.int32),
            vm((BLK, 128), F32),
            vm((2, 2, QR, KVC), BF),
            vm((2, 2, 4, 2, HALF, 128), BF),
            vm((2, 4, 2, HALF, 128), BF),
            vm((2, 2, HALF, 128), BF),
            vm((2, 2, 2, HALF, 128), BF),
            vm((2, HALF, 128), BF),
            vm((2, 2, 4, 2, HALF, 128), BF),
            vm((2, BLK, 128), F32),
            vm((2, BLK, 128), F32),
            vm((TOK, D), BF),
            vm((TOK, INNER), BF),
            vm((4, TOK, BLK), BF),
            vm((TOK, INNER), BF),
            vm((D, INNER), BF),
            vm((4 * BLK, INNER), BF),
            vm((2, HALF, INNER), BF),
            vm((2, BLK, INNER), BF),
            vm((TOK, INNER), F32),
            pltpu.SemaphoreType.DMA((len(KEYS),)),
            pltpu.SemaphoreType.DMA((len(KEYS),)),
            pltpu.SemaphoreType.DMA((len(LOCAL),)),
        ],
        compiler_params=pltpu.CompilerParams(
            collective_id=0, has_side_effects=True, vmem_limit_bytes=44 << 20
        ),
        cost_estimate=pl.CostEstimate(
            flops=6 * TOK * D * INNER, bytes_accessed=26 << 20, transcendentals=0
        ),
        name="sync_and_layer",
    )(*(pltpu.with_memory_space_constraint(a, pltpu.HBM) for a in given))
    return pl.pallas_call(
        write_out,
        out_shape=tuple(jax.ShapeDtypeStruct(*out) for out in outs),
        in_specs=[vm_spec] * 6,
        out_specs=[any_spec] * 6,
        scratch_shapes=[pltpu.SemaphoreType.DMA((6,))],
        compiler_params=pltpu.CompilerParams(vmem_limit_bytes=1 << 20),
        name="write_out",
    )(*(pltpu.with_memory_space_constraint(r, vm) for r in results))


def solution(mesh):
    placed = (
        P("shard"),
        P(None, "rep", "shard", None),
        P(None, "shard", "rep"),
        P(None, "shard", "rep"),
        P("rep", "shard", None),
        P("rep", "shard", None),
        P("rep", "shard", None),
    )
    return jax.shard_map(
        body,
        mesh=mesh,
        in_specs=placed,
        out_specs=(
            P("shard", None),
            P("shard", "rep"),
            P("shard", "rep"),
            P("rep", "shard", None),
            P("rep", "shard", None),
            P("rep", "shard", None),
        ),
        check_vma=False,
    )
```

```python
import jax
import jax.numpy as jnp
from jax import lax
from jax.experimental import pallas as pl
from jax.experimental.pallas import tpu as pltpu
from jax.sharding import PartitionSpec as P

OUTER_LR = 0.7
OUTER_MU = 0.9
BF = jnp.bfloat16
F32 = jnp.float32
D, KVC, INNER, TOK = 8192, 2048, 512, 256
BLK = 1024
QR = 256
HALF = 512
QS = range(4)
HS = range(2)

KEYS = (
    [("og",)]
    + [("ax", k) for k in range(4)]
    + [("g1", w, q) for w in "SUD" for q in QS]
    + [("g2", w, q) for w, qs in (("U", (0, 1)), ("D", (2, 3))) for q in qs]
    + [("g3", w, q) for w in "UD" for q in QS]
    + [("g4", q) for q in (1, 2)]
    + [("g5", w) for w in "UD"]
    + [("rb", w, i) for w in "UD" for i in HS]
    + [("rc", w, q) for w in "UD" for q in QS]
    + [("c1", h) for h in HS]
    + [("zb", w) for w in "UD"]
    + [("zc", w, h) for w in "UD" for h in HS]
    + [("xr", h) for h in HS]
    + [("xp", h) for h in HS]
    + [("zp", w, h) for w in "UD" for h in HS]
    + [("zf", w) for w in "UD"]
    + [("c2", k, h) for k in range(4) for h in HS]
)
SEM = {key: i for i, key in enumerate(KEYS)}
LOCAL = (
    ["og", "plan", "w", "mast", "mom", "np"]
    + [("act", j) for j in range(8)]
    + [("lp", k) for k in QS]
)
LSEM = {key: i for i, key in enumerate(LOCAL)}


def kernel(
    plan_h, lp_h, mast_h, mom_h, w_h, act_h, og_h,
    np_o, nm, nmo, keys_o, ig, wg_o,
    plan_v, pick, lpb, sel, cr, zb, zc, xr, npv, mast, mom,
    act, og, acts, ogs, wg, tt, rb, rc, acc,
    ss, rs, ls, here,
):
    rep, shard = lax.axis_index("rep"), lax.axis_index("shard")
    z, xl, c = rep // 4, (rep // 2) % 2, rep % 2
    y, xh = shard // 2, shard % 2
    yu, yd, yo = (y + 1) % 4, (y + 3) % 4, (y + 2) % 4
    zu, zd, zo = (z + 1) % 4, (z + 3) % 4, (z + 2) % 4
    me, sib = shard, y * 2 + 1 - xh
    bu, bd, bo = yu * 2 + xh, yd * 2 + xh, yo * 2 + xh
    bus, bds, bos = yu * 2 + 1 - xh, yd * 2 + 1 - xh, yo * 2 + 1 - xh
    to = {
        "U": (rep, bu), "D": (rep, bd), "S": (rep, sib),
        "X": (z * 4 + (1 - xl) * 2 + c, shard), "C": (z * 4 + xl * 2 + 1 - c, shard),
        "ZU": (zu * 4 + xl * 2 + c, shard), "ZD": (zd * 4 + xl * 2 + c, shard),
    }
    started = []

    def send(src, dst, key, way):
        copy = pltpu.make_async_remote_copy(
            src_ref=src, dst_ref=dst, send_sem=ss.at[SEM[key]], recv_sem=rs.at[SEM[key]],
            device_id=to[way], device_id_type=pl.DeviceIdType.MESH,
        )
        copy.start()
        started.append(copy)

    def arrived(dst, key, way):
        pltpu.make_async_remote_copy(
            src_ref=dst, dst_ref=dst, send_sem=ss.at[SEM[key]], recv_sem=rs.at[SEM[key]],
            device_id=to[way], device_id_type=pl.DeviceIdType.MESH,
        ).wait_recv()

    def fetch(src, dst, key):
        copy = pltpu.make_async_copy(src, dst, ls.at[LSEM[key]])
        copy.start()
        return copy

    def rows(block, q=0, n=QR):
        return pl.ds(pl.multiple_of(block * BLK + q * QR, QR), n)

    def cols(block, i=0, n=BLK):
        return pl.ds(pl.multiple_of(block * BLK + i, QR), n)

    barrier = pltpu.get_barrier_semaphore()

    def signal(semaphore, way):
        pl.semaphore_signal(semaphore, inc=1, device_id=to[way], device_id_type=pl.DeviceIdType.MESH)

    for way in ("U", "D", "S", "X", "C"):
        signal(barrier, way)
    pl.when(z < 3)(lambda: signal(barrier, "ZU"))
    pl.when(z == 0)(lambda: signal(barrier, "ZD"))
    pl.semaphore_wait(barrier, 5 + jnp.where(z == 0, 0, jnp.where(z == 3, 2, 1)))
    pl.when(z > 0)(lambda: signal(here, "ZD"))
    pl.when(z == 3)(lambda: signal(here, "ZU"))

    def tokens_to_sibling(k):
        yy = (yo, yu, yd, y)[k]
        send(act_h.at[0, :, cols(yy * 2 + 1 - xh)], acts.at[yy], ("ax", k), "S")

    def weight_to(w, q):
        send(w_h.at[0, pl.ds(q * QR, QR)], wg.at[rows(me, q)], ("g1", w, q), w)

    def weight_to_sibling(q):
        weight_to("S", q)

    for q in QS:
        weight_to("U", q)
        weight_to("D", 3 - q)
        if q == 0:
            send(og_h.at[0], ogs, ("og",), "S")
            tokens_to_sibling(0)
    tokens_to_sibling(1)
    tokens_to_sibling(2)

    f_plan = fetch(plan_h, plan_v, "plan")
    f_lp = [
        fetch(lp_h.at[:, 0, pl.ds(k * QR, QR)], lpb.at[k % 2], ("lp", k)) for k in (0, 1)
    ]
    f_og = fetch(og_h.at[0], og, "og")
    f_w = fetch(w_h.at[0], wg.at[rows(me, 0, BLK)], "w")
    order = [me, bo, bu, bd, bus, bds, bos, sib]
    f_act = [fetch(act_h.at[0, :, cols(j)], act.at[:, cols(j)], ("act", i)) for i, j in enumerate(order)]
    f_mast = fetch(mast_h, mast, "mast")
    f_mom = fetch(mom_h, mom, "mom")


    f_plan.wait()
    for g in range(8):
        line = plan_v[pl.ds(g, 1), :].astype(F32)
        pick[pl.ds(g * 128, 128), :] = jnp.broadcast_to(line, (128, 128)).T

    for k in QS:
        f_lp[k].wait()

        def choose(i, _, k=k):
            r = pl.multiple_of(i * 64, 64)
            mask = pick[pl.ds(k * QR + r, 64), :] == 1.0
            for b in range(16):
                a0 = lpb[k % 2, 0, pl.ds(r, 64), b * 128 : (b + 1) * 128].astype(F32)
                a1 = lpb[k % 2, 1, pl.ds(r, 64), b * 128 : (b + 1) * 128].astype(F32)
                sel[b % 2, k // 2, b // 4, (b // 2) % 2, pl.ds((k % 2) * QR + r, 64), :] = jnp.where(
                    mask, a1, a0
                ).astype(BF)
            return 0

        lax.fori_loop(0, 4, choose, 0)
        if k < 2:
            f_lp.append(
                fetch(lp_h.at[:, 0, pl.ds((k + 2) * QR, QR)], lpb.at[k % 2], ("lp", k + 2))
            )
        if k % 2 == 1:
            send(sel.at[1 - c, k // 2], cr.at[k // 2], ("c1", k // 2), "C")

    f_og.wait()
    acc[...] = jnp.zeros_like(acc)

    def layer(block, q0=0, n=4):
        def sub(i, _):
            at = cols(block, (q0 + i) * QR, QR)
            w = wg[at, :]
            acc[...] += jnp.dot(act[:, at], w, preferred_element_type=F32)
            ig[0, :, at] = lax.dot_general(
                og[...], w, (((1,), (1,)), ((), ())), preferred_element_type=F32
            ).astype(BF)
            return 0

        lax.fori_loop(0, n, sub, 0)

    def term(k):
        yy = (yo, yu, yd, y)[k]
        arrived(acts.at[yy], ("ax", k), "S")
        if k == 0:
            weight_to_sibling(0)

        def sub(i, _):
            at = pl.ds(pl.multiple_of(i * QR, QR), QR)
            over_tokens = (((0,), (0,)), ((), ()))
            t = lax.dot_general(
                act[:, cols(yy * 2 + xh, i * QR, QR)], og[...], over_tokens, preferred_element_type=F32
            ) + lax.dot_general(acts[yy, :, at], ogs[...], over_tokens, preferred_element_type=F32)
            tt[rows(yy, i), :] = t.astype(BF)
            return 0

        lax.fori_loop(0, 4, sub, 0)

    def add_into(dst, dst_row, *sources):
        def sub(i, _):
            at = pl.ds(pl.multiple_of(dst_row + i * 64, 64), 64)
            total = dst[at, :].astype(F32)
            for ref, row in sources:
                total = total + ref[pl.ds(row + i * 64, 64), :].astype(F32)
            dst[at, :] = total.astype(BF)
            return 0

        lax.fori_loop(0, QR // 64, sub, 0)

    f_w.wait()
    for copy in f_act:
        copy.wait()
    layer(me)

    def core_sum(zz, h):
        def sub(i, _):
            at = pl.ds(pl.multiple_of(i * 128, 128), 128)
            for l in HS:
                sel[c, h, zz, l, at, :] = (
                    sel[c, h, zz, l, at, :].astype(F32) + cr[h, zz, l, at, :].astype(F32)
                ).astype(BF)
            return 0

        lax.fori_loop(0, 4, sub, 0)

    for h in HS:
        arrived(cr.at[h], ("c1", h), "C")
    core_sum(zo, 0)
    pl.when(z < 3)(lambda: pl.semaphore_wait(here, jnp.where(z == 0, 2, 1)))
    send(sel.at[c, 0, zo], zb.at[1], ("zb", "D"), "ZD")
    core_sum(zo, 1)
    send(sel.at[c, 1, zo], zb.at[0], ("zb", "U"), "ZU")
    core_sum(zu, 0)
    send(sel.at[c, 0, zu], zc.at[0, 0], ("zc", "U", 0), "ZU")
    core_sum(zd, 1)
    send(sel.at[c, 1, zd], zc.at[1, 1], ("zc", "D", 1), "ZD")
    core_sum(zu, 1)
    core_sum(zd, 0)
    core_sum(z, 0)
    core_sum(z, 1)

    for q in (0, 1):
        arrived(wg.at[rows(bd, q)], ("g1", "U", q), "D")
        send(wg.at[rows(bd, q)], wg.at[rows(bd, q)], ("g2", "U", q), "U")
        arrived(wg.at[rows(bu, 3 - q)], ("g1", "D", 3 - q), "U")
        send(wg.at[rows(bu, 3 - q)], wg.at[rows(bu, 3 - q)], ("g2", "D", 3 - q), "D")

    arrived(ogs, ("og",), "S")
    term(0)
    for q in (0, 2, 1, 3):
        way = "D" if q < 2 else "U"
        side = 1 if q < 2 else 0
        send(tt.at[rows(yo, q)], rb.at[side, pl.ds((q % 2) * QR, QR)], ("rb", way, q % 2), way)

    def z_add(h, zz, way):
        def sub(i, _):
            at = pl.ds(pl.multiple_of(i * 128, 128), 128)
            for l in HS:
                sel[c, h, zz, l, at, :] = (
                    sel[c, h, zz, l, at, :].astype(F32) + zb[way, l, at, :].astype(F32)
                ).astype(BF)
            return 0

        lax.fori_loop(0, 4, sub, 0)

    arrived(zb.at[0], ("zb", "U"), "ZD")
    z_add(1, zu, 0)
    send(sel.at[c, 1, zu], zc.at[0, 1], ("zc", "U", 1), "ZU")
    arrived(zb.at[1], ("zb", "D"), "ZU")
    z_add(0, zd, 1)
    send(sel.at[c, 0, zd], zc.at[1, 0], ("zc", "D", 0), "ZD")

    term(1)
    for q in (0, 1):
        send(tt.at[rows(yu, q)], rc.at[0, pl.ds(q * QR, QR)], ("rc", "U", q), "U")

    for h in HS:
        arrived(zc.at[0, h], ("zc", "U", h), "ZD")
        arrived(zc.at[1, h], ("zc", "D", h), "ZU")

        def z_sum(i, _, h=h):
            at = pl.ds(pl.multiple_of(i * 128, 128), 128)
            sel[c, h, z, 1 - xl, at, :] = (
                sel[c, h, z, 1 - xl, at, :].astype(F32)
                + zc[0, h, 1 - xl, at, :].astype(F32)
                + zc[1, h, 1 - xl, at, :].astype(F32)
            ).astype(BF)
            return 0

        lax.fori_loop(0, 4, z_sum, 0)
        send(sel.at[c, h, z, 1 - xl], xr.at[h], ("xr", h), "X")

    weight_to_sibling(3)
    for q in (2, 3):
        arrived(wg.at[rows(bd, q)], ("g1", "U", q), "D")
        arrived(wg.at[rows(bu, 3 - q)], ("g1", "D", 3 - q), "U")
    layer(bd)
    layer(bu)

    term(2)
    for q in (2, 3):
        send(tt.at[rows(yd, q)], rc.at[1, pl.ds(q * QR, QR)], ("rc", "D", q), "D")

    for i in HS:
        q = 2 + i
        arrived(rb.at[0, pl.ds(i * QR, QR)], ("rb", "U", i), "D")
        add_into(tt, yu * BLK + q * QR, (rb.at[0], i * QR))
        send(tt.at[rows(yu, q)], rc.at[0, pl.ds(q * QR, QR)], ("rc", "U", q), "U")
        arrived(rb.at[1, pl.ds(i * QR, QR)], ("rb", "D", i), "U")
        add_into(tt, yd * BLK + i * QR, (rb.at[1], i * QR))
        send(tt.at[rows(yd, i)], rc.at[1, pl.ds(i * QR, QR)], ("rc", "D", i), "D")

    f_mast.wait()
    f_mom.wait()
    for h in HS:
        arrived(xr.at[h], ("xr", h), "X")

        def update(i, _, h=h):
            at = pl.ds(pl.multiple_of(i * 64, 64), 64)
            to_row = pl.ds(pl.multiple_of(h * HALF + i * 64, 64), 64)
            total = (
                sel[c, h, z, xl, at, :].astype(F32)
                + zc[0, h, xl, at, :].astype(F32)
                + zc[1, h, xl, at, :].astype(F32)
                + xr[h, at, :].astype(F32)
            )
            mask = pick[to_row, :] == 1.0
            master_now = jnp.where(mask, mast[1, to_row, :], mast[0, to_row, :])
            moment_now = jnp.where(mask, mom[1, to_row, :], mom[0, to_row, :])
            outer_grad = master_now - total / 16
            new_momentum = OUTER_MU * moment_now + outer_grad
            new_master = master_now - OUTER_LR * (outer_grad + OUTER_MU * new_momentum)
            nmo[to_row, :] = new_momentum
            nm[to_row, :] = new_master
            npv[c, h, z, xl, at, :] = new_master.astype(BF)
            return 0

        lax.fori_loop(0, 8, update, 0)
        send(npv.at[c, h, z, xl], npv.at[c, h, z, xl], ("xp", h), "X")

    for q in (1, 2):
        weight_to_sibling(q)
    tokens_to_sibling(3)

    for q in QS:
        way, back = ("U", "D") if q < 2 else ("D", "U")
        arrived(wg.at[rows(bo, q)], ("g2", way, q), back)
        if q in (1, 2):
            send(wg.at[rows(bo, q)], wg.at[rows(bo, q)], ("g4", q), "S")
    layer(bo)

    def pass_on(q):
        arrived(wg.at[rows(sib, q)], ("g1", "S", q), "S")
        for w in "UD":
            send(wg.at[rows(sib, q)], wg.at[rows(sib, q)], ("g3", w, q), w)

    pass_on(0)

    for h in HS:
        arrived(npv.at[c, h, z, 1 - xl], ("xp", h), "X")
        for w in "UD":
            send(npv.at[c, h, z], npv.at[c, h, z], ("zp", w, h), "Z" + w)
        send(npv.at[c, h, z], npv.at[c, h, z], ("c2", 0, h), "C")

    for h in HS:
        pass_on((3, 1)[h])
        arrived(npv.at[c, h, zd], ("zp", "U", h), "ZD")
        if h == 0:
            send(npv.at[c, 0, zd], npv.at[c, 0, zd], ("zf", "U"), "ZU")
        send(npv.at[c, h, zd], npv.at[c, h, zd], ("c2", 1, h), "C")
        arrived(npv.at[c, h, zu], ("zp", "D", h), "ZU")
        if h == 1:
            send(npv.at[c, 1, zu], npv.at[c, 1, zu], ("zf", "D"), "ZD")
        send(npv.at[c, h, zu], npv.at[c, h, zu], ("c2", 2, h), "C")
    pass_on(2)

    arrived(wg.at[rows(bds, 0)], ("g3", "U", 0), "D")
    send(wg.at[rows(bds, 0)], wg.at[rows(bds, 0)], ("g5", "U"), "U")
    arrived(wg.at[rows(bus, 3)], ("g3", "D", 3), "U")
    send(wg.at[rows(bus, 3)], wg.at[rows(bus, 3)], ("g5", "D"), "D")

    arrived(npv.at[c, 0, zo], ("zf", "U"), "ZD")
    send(npv.at[c, 0, zo], npv.at[c, 0, zo], ("c2", 3, 0), "C")
    arrived(npv.at[c, 1, zo], ("zf", "D"), "ZU")
    send(npv.at[c, 1, zo], npv.at[c, 1, zo], ("c2", 3, 1), "C")

    layer(sib)

    term(3)
    for q in QS:
        arrived(rc.at[0, pl.ds(q * QR, QR)], ("rc", "U", q), "D")
        arrived(rc.at[1, pl.ds(q * QR, QR)], ("rc", "D", q), "U")

        def grad_sum(i, _, q=q):
            at = pl.ds(pl.multiple_of(q * QR + i * 64, 64), 64)
            wg_o[0, at, :] = (
                tt[pl.ds(pl.multiple_of(y * BLK + q * QR + i * 64, 64), 64), :].astype(F32)
                + rc[0, at, :].astype(F32)
                + rc[1, at, :].astype(F32)
            ).astype(BF)
            return 0

        lax.fori_loop(0, 4, grad_sum, 0)

    for h in HS:
        for k, zz in enumerate((z, zd, zu, zo)):
            arrived(npv.at[1 - c, h, zz], ("c2", k, h), "C")
    for b in range(16):
        for h in HS:
            pltpu.make_async_copy(
                npv.at[b % 2, h, b // 4, (b // 2) % 2],
                np_o.at[pl.ds(h * HALF, HALF), pl.ds(b * 128, 128)],
                ls.at[LSEM["np"]],
            ).start()

    layer(bds, 0, 1)
    layer(bus, 3, 1)
    arrived(wg.at[rows(bds, 3)], ("g3", "U", 3), "D")
    layer(bds, 3, 1)
    arrived(wg.at[rows(bus, 0)], ("g3", "D", 0), "U")
    layer(bus, 0, 1)
    pltpu.make_async_copy(np_o, np_o, ls.at[LSEM["np"]]).wait()
    last = 16
    for q in (1, 2):
        arrived(wg.at[rows(bos, q)], ("g4", q), "S")
        arrived(wg.at[rows(bds, q)], ("g3", "U", q), "D")
        arrived(wg.at[rows(bus, q)], ("g3", "D", q), "U")
        for block in (bos, bds, bus):
            layer(block, q, 1)
        if q == 1:
            for copy in started[:-last]:
                copy.wait_send()
    arrived(wg.at[rows(bos, 0)], ("g5", "U"), "D")
    layer(bos, 0, 1)
    arrived(wg.at[rows(bos, 3)], ("g5", "D"), "U")
    layer(bos, 3, 1)
    keys_o[0] = acc[...].astype(BF)
    for copy in started[-last:]:
        copy.wait_send()


def write_out(*refs):
    n = len(refs) // 2
    sems = refs[-1]
    copies = [pltpu.make_async_copy(refs[i], refs[n + i], sems.at[i]) for i in range(n)]
    for copy in copies:
        copy.start()
    for copy in copies:
        copy.wait()


def body(plan, local_params, master, momentum, inner_weight, activations, out_grad):
    vm = pltpu.VMEM
    any_spec = pl.BlockSpec(memory_space=pl.ANY)
    vm_spec = pl.BlockSpec(memory_space=vm)
    outs = (
        ((BLK, KVC), BF),
        ((BLK, 128), F32),
        ((BLK, 128), F32),
        ((1, TOK, INNER), BF),
        ((1, TOK, D), BF),
        ((1, BLK, INNER), BF),
    )
    given = (plan.reshape(8, 128), local_params, master, momentum, inner_weight, activations, out_grad)
    results = pl.pallas_call(
        kernel,
        out_shape=tuple(vm(*out) for out in outs),
        in_specs=[any_spec] * 7,
        out_specs=[vm_spec] * 6,
        scratch_shapes=[
            vm((8, 128), jnp.int32),
            vm((BLK, 128), F32),
            vm((2, 2, QR, KVC), BF),
            vm((2, 2, 4, 2, HALF, 128), BF),
            vm((2, 4, 2, HALF, 128), BF),
            vm((2, 2, HALF, 128), BF),
            vm((2, 2, 2, HALF, 128), BF),
            vm((2, HALF, 128), BF),
            vm((2, 2, 4, 2, HALF, 128), BF),
            vm((2, BLK, 128), F32),
            vm((2, BLK, 128), F32),
            vm((TOK, D), BF),
            vm((TOK, INNER), BF),
            vm((4, TOK, BLK), BF),
            vm((TOK, INNER), BF),
            vm((D, INNER), BF),
            vm((4 * BLK, INNER), BF),
            vm((2, HALF, INNER), BF),
            vm((2, BLK, INNER), BF),
            vm((TOK, INNER), F32),
            pltpu.SemaphoreType.DMA((len(KEYS),)),
            pltpu.SemaphoreType.DMA((len(KEYS),)),
            pltpu.SemaphoreType.DMA((len(LOCAL),)),
            pltpu.SemaphoreType.REGULAR,
        ],
        compiler_params=pltpu.CompilerParams(
            collective_id=0, has_side_effects=True, vmem_limit_bytes=44 << 20
        ),
        cost_estimate=pl.CostEstimate(
            flops=6 * TOK * D * INNER, bytes_accessed=26 << 20, transcendentals=0
        ),
        name="sync_and_layer",
    )(*(pltpu.with_memory_space_constraint(a, pltpu.HBM) for a in given))
    return pl.pallas_call(
        write_out,
        out_shape=tuple(jax.ShapeDtypeStruct(*out) for out in outs),
        in_specs=[vm_spec] * 6,
        out_specs=[any_spec] * 6,
        scratch_shapes=[pltpu.SemaphoreType.DMA((6,))],
        compiler_params=pltpu.CompilerParams(vmem_limit_bytes=1 << 20),
        name="write_out",
    )(*(pltpu.with_memory_space_constraint(r, vm) for r in results))


def solution(mesh):
    placed = (
        P("shard"),
        P(None, "rep", "shard", None),
        P(None, "shard", "rep"),
        P(None, "shard", "rep"),
        P("rep", "shard", None),
        P("rep", "shard", None),
        P("rep", "shard", None),
    )
    return jax.shard_map(
        body,
        mesh=mesh,
        in_specs=placed,
        out_specs=(
            P("shard", None),
            P("shard", "rep"),
            P("shard", "rep"),
            P("rep", "shard", None),
            P("rep", "shard", None),
            P("rep", "shard", None),
        ),
        check_vma=False,
    )
```

```python
import jax
import jax.numpy as jnp
from jax import lax
from jax.experimental import pallas as pl
from jax.experimental.pallas import tpu as pltpu
from jax.sharding import PartitionSpec as P

OUTER_LR = 0.7
OUTER_MU = 0.9
BF = jnp.bfloat16
F32 = jnp.float32
D, KVC, INNER, TOK = 8192, 2048, 512, 256
BLK = 1024
QR = 256
HALF = 512
QS = range(4)
HS = range(2)

KEYS = (
    [("og",)]
    + [("ax", k) for k in range(4)]
    + [("g1", w, q) for w in "SUD" for q in QS]
    + [("g2", w, q) for w, qs in (("U", (0, 1)), ("D", (2, 3))) for q in qs]
    + [("g3", w, q) for w in "UD" for q in QS]
    + [("g4", q) for q in (1, 2)]
    + [("g5", w) for w in "UD"]
    + [("rb", w, i) for w in "UD" for i in HS]
    + [("rc", w, q) for w in "UD" for q in QS]
    + [("c1", h) for h in HS]
    + [("zb", w) for w in "UD"]
    + [("zc", w, h) for w in "UD" for h in HS]
    + [("xr", h) for h in HS]
    + [("xp", h) for h in HS]
    + [("zp", w, h) for w in "UD" for h in HS]
    + [("zf", w) for w in "UD"]
    + [("c2", k, h) for k in range(4) for h in HS]
)
SEM = {key: i for i, key in enumerate(KEYS)}
LATE = (("g4", 2), ("g5", "U"), ("g5", "D"), ("g3", "U", 2), ("g3", "D", 2))
LOCAL = (
    ["og", "plan", "w", "mast", "mom", "np"]
    + [("act", j) for j in range(8)]
    + [("lp", k) for k in QS]
)
LSEM = {key: i for i, key in enumerate(LOCAL)}


def kernel(
    plan_h, lp_h, mast_h, mom_h, w_h, act_h, og_h,
    np_o, nm, nmo, keys_o, ig, wg_o,
    plan_v, pick, lpb, sel, cr, zb, zc, xr, npv, mast, mom,
    act, og, acts, ogs, wg, tt, rb, rc, acc,
    ss, rs, ls, here,
):
    rep, shard = lax.axis_index("rep"), lax.axis_index("shard")
    z, xl, c = rep // 4, (rep // 2) % 2, rep % 2
    y, xh = shard // 2, shard % 2
    yu, yd, yo = (y + 1) % 4, (y + 3) % 4, (y + 2) % 4
    zu, zd, zo = (z + 1) % 4, (z + 3) % 4, (z + 2) % 4
    me, sib = shard, y * 2 + 1 - xh
    bu, bd, bo = yu * 2 + xh, yd * 2 + xh, yo * 2 + xh
    bus, bds, bos = yu * 2 + 1 - xh, yd * 2 + 1 - xh, yo * 2 + 1 - xh
    to = {
        "U": (rep, bu), "D": (rep, bd), "S": (rep, sib),
        "X": (z * 4 + (1 - xl) * 2 + c, shard), "C": (z * 4 + xl * 2 + 1 - c, shard),
        "ZU": (zu * 4 + xl * 2 + c, shard), "ZD": (zd * 4 + xl * 2 + c, shard),
    }
    started, late = [], []

    def remote(src, dst, key, way):
        return pltpu.make_async_remote_copy(
            src_ref=src, dst_ref=dst, send_sem=ss.at[SEM[key]], recv_sem=rs.at[SEM[key]],
            device_id=to[way], device_id_type=pl.DeviceIdType.MESH,
        )

    def send(src, dst, key, way):
        remote(src, dst, key, way).start()
        (late if key in LATE else started).append((src, dst, key, way))

    def arrived(dst, key, way):
        remote(dst, dst, key, way).wait_recv()

    def fetch(src, dst, key):
        copy = pltpu.make_async_copy(src, dst, ls.at[LSEM[key]])
        copy.start()
        return copy

    def rows(block, q=0, n=QR):
        return pl.ds(pl.multiple_of(block * BLK + q * QR, QR), n)

    def cols(block, i=0, n=BLK):
        return pl.ds(pl.multiple_of(block * BLK + i, QR), n)

    barrier = pltpu.get_barrier_semaphore()

    def signal(semaphore, way):
        pl.semaphore_signal(semaphore, inc=1, device_id=to[way], device_id_type=pl.DeviceIdType.MESH)

    before = {
        "U": y == 3, "D": y > 0, "S": xh == 1, "X": xl == 1, "ZU": z == 3, "ZD": z > 0,
    }
    back_of = {"U": "D", "D": "U", "S": "S", "X": "X", "ZU": "ZD", "ZD": "ZU"}
    slot = {way: i for i, way in enumerate(before)}
    signal(barrier, "C")
    for way, first in before.items():
        pl.when(jnp.logical_not(first))(lambda way=way: signal(barrier, way))
    expected = 1
    for first in before.values():
        expected = expected + jnp.where(first, 1, 0)
    pl.semaphore_wait(barrier, expected)
    for way, first in before.items():
        pl.when(first)(lambda way=way: signal(here.at[slot[back_of[way]]], way))

    def answered(way):
        pl.when(jnp.logical_not(before[way]))(lambda: pl.semaphore_wait(here.at[slot[way]], 1))

    def tokens(k):
        yy = (yo, yu, yd, y)[k]
        return act_h.at[0, :, cols(yy * 2 + 1 - xh)], acts.at[yy], ("ax", k), "S"

    def weight(w, q):
        return w_h.at[0, pl.ds(q * QR, QR)], wg.at[rows(me, q)], ("g1", w, q), w

    def tokens_to_sibling(k):
        send(*tokens(k))

    def weight_to_sibling(q):
        send(*weight("S", q))

    def first_copies(way):
        if way == "S":
            return [(og_h.at[0], ogs, ("og",), "S")] + [tokens(k) for k in range(3)]
        return [weight(way, q) for q in ((0, 1, 2, 3) if way == "U" else (3, 2, 1, 0))]

    def first_sends(way):
        for copy in first_copies(way):
            remote(*copy).start()

    for way in ("U", "D", "S"):
        pl.when(before[way])(lambda way=way: first_sends(way))
    for way in ("U", "S", "D"):

        @pl.when(jnp.logical_not(before[way]))
        def _(way=way):
            pl.semaphore_wait(here.at[slot[way]], 1)
            first_sends(way)

        started.extend(first_copies(way))

    f_plan = fetch(plan_h, plan_v, "plan")
    f_lp = [
        fetch(lp_h.at[:, 0, pl.ds(k * QR, QR)], lpb.at[k % 2], ("lp", k)) for k in (0, 1)
    ]
    f_og = fetch(og_h.at[0], og, "og")
    f_w = fetch(w_h.at[0], wg.at[rows(me, 0, BLK)], "w")
    order = [me, bo, bu, bd, bus, bds, bos, sib]
    f_act = [fetch(act_h.at[0, :, cols(j)], act.at[:, cols(j)], ("act", i)) for i, j in enumerate(order)]
    f_mast = fetch(mast_h, mast, "mast")
    f_mom = fetch(mom_h, mom, "mom")


    f_plan.wait()
    for g in range(8):
        line = plan_v[pl.ds(g, 1), :].astype(F32)
        pick[pl.ds(g * 128, 128), :] = jnp.broadcast_to(line, (128, 128)).T

    for k in QS:
        f_lp[k].wait()

        def choose(i, _, k=k):
            r = pl.multiple_of(i * 64, 64)
            mask = pick[pl.ds(k * QR + r, 64), :] == 1.0
            for b in range(16):
                a0 = lpb[k % 2, 0, pl.ds(r, 64), b * 128 : (b + 1) * 128].astype(F32)
                a1 = lpb[k % 2, 1, pl.ds(r, 64), b * 128 : (b + 1) * 128].astype(F32)
                sel[b % 2, k // 2, b // 4, (b // 2) % 2, pl.ds((k % 2) * QR + r, 64), :] = jnp.where(
                    mask, a1, a0
                ).astype(BF)
            return 0

        lax.fori_loop(0, 4, choose, 0)
        if k < 2:
            f_lp.append(
                fetch(lp_h.at[:, 0, pl.ds((k + 2) * QR, QR)], lpb.at[k % 2], ("lp", k + 2))
            )
        if k % 2 == 1:
            send(sel.at[1 - c, k // 2], cr.at[k // 2], ("c1", k // 2), "C")

    f_og.wait()
    acc[...] = jnp.zeros_like(acc)

    def layer(block, q0=0, n=4):
        def sub(i, _):
            at = cols(block, (q0 + i) * QR, QR)
            w = wg[at, :]
            acc[...] += jnp.dot(act[:, at], w, preferred_element_type=F32)
            ig[0, :, at] = lax.dot_general(
                og[...], w, (((1,), (1,)), ((), ())), preferred_element_type=F32
            ).astype(BF)
            return 0

        lax.fori_loop(0, n, sub, 0)

    def term(k):
        yy = (yo, yu, yd, y)[k]
        arrived(acts.at[yy], ("ax", k), "S")
        if k == 0:
            weight_to_sibling(0)

        def sub(i, _):
            at = pl.ds(pl.multiple_of(i * QR, QR), QR)
            over_tokens = (((0,), (0,)), ((), ()))
            t = lax.dot_general(
                act[:, cols(yy * 2 + xh, i * QR, QR)], og[...], over_tokens, preferred_element_type=F32
            ) + lax.dot_general(acts[yy, :, at], ogs[...], over_tokens, preferred_element_type=F32)
            tt[rows(yy, i), :] = t.astype(BF)
            return 0

        lax.fori_loop(0, 4, sub, 0)

    def add_into(dst, dst_row, *sources):
        def sub(i, _):
            at = pl.ds(pl.multiple_of(dst_row + i * 64, 64), 64)
            total = dst[at, :].astype(F32)
            for ref, row in sources:
                total = total + ref[pl.ds(row + i * 64, 64), :].astype(F32)
            dst[at, :] = total.astype(BF)
            return 0

        lax.fori_loop(0, QR // 64, sub, 0)

    f_w.wait()
    for copy in f_act:
        copy.wait()
    layer(me)

    def core_sum(zz, h):
        def sub(i, _):
            at = pl.ds(pl.multiple_of(i * 128, 128), 128)
            for l in HS:
                sel[c, h, zz, l, at, :] = (
                    sel[c, h, zz, l, at, :].astype(F32) + cr[h, zz, l, at, :].astype(F32)
                ).astype(BF)
            return 0

        lax.fori_loop(0, 4, sub, 0)

    for h in HS:
        arrived(cr.at[h], ("c1", h), "C")
    core_sum(zo, 0)
    answered("ZU")
    answered("ZD")
    send(sel.at[c, 0, zo], zb.at[1], ("zb", "D"), "ZD")
    core_sum(zo, 1)
    send(sel.at[c, 1, zo], zb.at[0], ("zb", "U"), "ZU")
    core_sum(zu, 0)
    send(sel.at[c, 0, zu], zc.at[0, 0], ("zc", "U", 0), "ZU")
    core_sum(zd, 1)
    send(sel.at[c, 1, zd], zc.at[1, 1], ("zc", "D", 1), "ZD")
    core_sum(zu, 1)
    core_sum(zd, 0)
    core_sum(z, 0)
    core_sum(z, 1)

    for q in (0, 1):
        arrived(wg.at[rows(bd, q)], ("g1", "U", q), "D")
        send(wg.at[rows(bd, q)], wg.at[rows(bd, q)], ("g2", "U", q), "U")
        arrived(wg.at[rows(bu, 3 - q)], ("g1", "D", 3 - q), "U")
        send(wg.at[rows(bu, 3 - q)], wg.at[rows(bu, 3 - q)], ("g2", "D", 3 - q), "D")

    arrived(ogs, ("og",), "S")
    term(0)
    for q in (0, 2, 1, 3):
        way = "D" if q < 2 else "U"
        side = 1 if q < 2 else 0
        send(tt.at[rows(yo, q)], rb.at[side, pl.ds((q % 2) * QR, QR)], ("rb", way, q % 2), way)

    def z_add(h, zz, way):
        def sub(i, _):
            at = pl.ds(pl.multiple_of(i * 128, 128), 128)
            for l in HS:
                sel[c, h, zz, l, at, :] = (
                    sel[c, h, zz, l, at, :].astype(F32) + zb[way, l, at, :].astype(F32)
                ).astype(BF)
            return 0

        lax.fori_loop(0, 4, sub, 0)

    arrived(zb.at[0], ("zb", "U"), "ZD")
    z_add(1, zu, 0)
    send(sel.at[c, 1, zu], zc.at[0, 1], ("zc", "U", 1), "ZU")
    arrived(zb.at[1], ("zb", "D"), "ZU")
    z_add(0, zd, 1)
    send(sel.at[c, 0, zd], zc.at[1, 0], ("zc", "D", 0), "ZD")

    term(1)
    for q in (0, 1):
        send(tt.at[rows(yu, q)], rc.at[0, pl.ds(q * QR, QR)], ("rc", "U", q), "U")

    answered("X")
    for h in HS:
        arrived(zc.at[0, h], ("zc", "U", h), "ZD")
        arrived(zc.at[1, h], ("zc", "D", h), "ZU")

        def z_sum(i, _, h=h):
            at = pl.ds(pl.multiple_of(i * 128, 128), 128)
            sel[c, h, z, 1 - xl, at, :] = (
                sel[c, h, z, 1 - xl, at, :].astype(F32)
                + zc[0, h, 1 - xl, at, :].astype(F32)
                + zc[1, h, 1 - xl, at, :].astype(F32)
            ).astype(BF)
            return 0

        lax.fori_loop(0, 4, z_sum, 0)
        send(sel.at[c, h, z, 1 - xl], xr.at[h], ("xr", h), "X")

    weight_to_sibling(3)
    for q in (2, 3):
        arrived(wg.at[rows(bd, q)], ("g1", "U", q), "D")
        arrived(wg.at[rows(bu, 3 - q)], ("g1", "D", 3 - q), "U")
    layer(bd)
    layer(bu)

    term(2)
    for q in (2, 3):
        send(tt.at[rows(yd, q)], rc.at[1, pl.ds(q * QR, QR)], ("rc", "D", q), "D")

    for i in HS:
        q = 2 + i
        arrived(rb.at[0, pl.ds(i * QR, QR)], ("rb", "U", i), "D")
        add_into(tt, yu * BLK + q * QR, (rb.at[0], i * QR))
        send(tt.at[rows(yu, q)], rc.at[0, pl.ds(q * QR, QR)], ("rc", "U", q), "U")
        arrived(rb.at[1, pl.ds(i * QR, QR)], ("rb", "D", i), "U")
        add_into(tt, yd * BLK + i * QR, (rb.at[1], i * QR))
        send(tt.at[rows(yd, i)], rc.at[1, pl.ds(i * QR, QR)], ("rc", "D", i), "D")

    f_mast.wait()
    f_mom.wait()
    for h in HS:
        arrived(xr.at[h], ("xr", h), "X")

        def update(i, _, h=h):
            at = pl.ds(pl.multiple_of(i * 64, 64), 64)
            to_row = pl.ds(pl.multiple_of(h * HALF + i * 64, 64), 64)
            total = (
                sel[c, h, z, xl, at, :].astype(F32)
                + zc[0, h, xl, at, :].astype(F32)
                + zc[1, h, xl, at, :].astype(F32)
                + xr[h, at, :].astype(F32)
            )
            mask = pick[to_row, :] == 1.0
            master_now = jnp.where(mask, mast[1, to_row, :], mast[0, to_row, :])
            moment_now = jnp.where(mask, mom[1, to_row, :], mom[0, to_row, :])
            outer_grad = master_now - total / 16
            new_momentum = OUTER_MU * moment_now + outer_grad
            new_master = master_now - OUTER_LR * (outer_grad + OUTER_MU * new_momentum)
            nmo[to_row, :] = new_momentum
            nm[to_row, :] = new_master
            npv[c, h, z, xl, at, :] = new_master.astype(BF)
            return 0

        lax.fori_loop(0, 8, update, 0)
        send(npv.at[c, h, z, xl], npv.at[c, h, z, xl], ("xp", h), "X")

    for q in (1, 2):
        weight_to_sibling(q)
    tokens_to_sibling(3)

    for q in QS:
        way, back = ("U", "D") if q < 2 else ("D", "U")
        arrived(wg.at[rows(bo, q)], ("g2", way, q), back)
        if q in (1, 2):
            send(wg.at[rows(bo, q)], wg.at[rows(bo, q)], ("g4", q), "S")
    layer(bo)

    def pass_on(q):
        arrived(wg.at[rows(sib, q)], ("g1", "S", q), "S")
        for w in "UD":
            send(wg.at[rows(sib, q)], wg.at[rows(sib, q)], ("g3", w, q), w)

    pass_on(0)

    for h in HS:
        arrived(npv.at[c, h, z, 1 - xl], ("xp", h), "X")
        for w in "UD":
            send(npv.at[c, h, z], npv.at[c, h, z], ("zp", w, h), "Z" + w)
        send(npv.at[c, h, z], npv.at[c, h, z], ("c2", 0, h), "C")

    for h in HS:
        pass_on((3, 1)[h])
        arrived(npv.at[c, h, zd], ("zp", "U", h), "ZD")
        if h == 0:
            send(npv.at[c, 0, zd], npv.at[c, 0, zd], ("zf", "U"), "ZU")
        send(npv.at[c, h, zd], npv.at[c, h, zd], ("c2", 1, h), "C")
        arrived(npv.at[c, h, zu], ("zp", "D", h), "ZU")
        if h == 1:
            send(npv.at[c, 1, zu], npv.at[c, 1, zu], ("zf", "D"), "ZD")
        send(npv.at[c, h, zu], npv.at[c, h, zu], ("c2", 2, h), "C")
    pass_on(2)

    arrived(wg.at[rows(bds, 0)], ("g3", "U", 0), "D")
    send(wg.at[rows(bds, 0)], wg.at[rows(bds, 0)], ("g5", "U"), "U")
    arrived(wg.at[rows(bus, 3)], ("g3", "D", 3), "U")
    send(wg.at[rows(bus, 3)], wg.at[rows(bus, 3)], ("g5", "D"), "D")

    arrived(npv.at[c, 0, zo], ("zf", "U"), "ZD")
    send(npv.at[c, 0, zo], npv.at[c, 0, zo], ("c2", 3, 0), "C")
    arrived(npv.at[c, 1, zo], ("zf", "D"), "ZU")
    send(npv.at[c, 1, zo], npv.at[c, 1, zo], ("c2", 3, 1), "C")

    layer(sib)

    term(3)
    for q in QS:
        arrived(rc.at[0, pl.ds(q * QR, QR)], ("rc", "U", q), "D")
        arrived(rc.at[1, pl.ds(q * QR, QR)], ("rc", "D", q), "U")

        def grad_sum(i, _, q=q):
            at = pl.ds(pl.multiple_of(q * QR + i * 64, 64), 64)
            wg_o[0, at, :] = (
                tt[pl.ds(pl.multiple_of(y * BLK + q * QR + i * 64, 64), 64), :].astype(F32)
                + rc[0, at, :].astype(F32)
                + rc[1, at, :].astype(F32)
            ).astype(BF)
            return 0

        lax.fori_loop(0, 4, grad_sum, 0)

    for h in HS:
        for k, zz in enumerate((z, zd, zu, zo)):
            arrived(npv.at[1 - c, h, zz], ("c2", k, h), "C")
    for b in range(16):
        for h in HS:
            pltpu.make_async_copy(
                npv.at[b % 2, h, b // 4, (b // 2) % 2],
                np_o.at[pl.ds(h * HALF, HALF), pl.ds(b * 128, 128)],
                ls.at[LSEM["np"]],
            ).start()

    layer(bds, 0, 1)
    layer(bus, 3, 1)
    arrived(wg.at[rows(bds, 3)], ("g3", "U", 3), "D")
    layer(bds, 3, 1)
    arrived(wg.at[rows(bus, 0)], ("g3", "D", 0), "U")
    layer(bus, 0, 1)
    pltpu.make_async_copy(np_o, np_o, ls.at[LSEM["np"]]).wait()
    for q in (1, 2):
        arrived(wg.at[rows(bds, q)], ("g3", "U", q), "D")
        layer(bds, q, 1)
        arrived(wg.at[rows(bus, q)], ("g3", "D", q), "U")
        layer(bus, q, 1)
    arrived(wg.at[rows(bos, 1)], ("g4", 1), "S")
    layer(bos, 1, 1)
    for copy in started:
        remote(*copy).wait_send()
    arrived(wg.at[rows(bos, 0)], ("g5", "U"), "D")
    layer(bos, 0, 1)
    arrived(wg.at[rows(bos, 3)], ("g5", "D"), "U")
    layer(bos, 3, 1)
    arrived(wg.at[rows(bos, 2)], ("g4", 2), "S")
    layer(bos, 2, 1)
    keys_o[0] = acc[...].astype(BF)
    for copy in late:
        remote(*copy).wait_send()


def write_out(*refs):
    n = len(refs) // 2
    sems = refs[-1]
    copies = [pltpu.make_async_copy(refs[i], refs[n + i], sems.at[i]) for i in range(n)]
    for copy in copies:
        copy.start()
    for copy in copies:
        copy.wait()


def body(plan, local_params, master, momentum, inner_weight, activations, out_grad):
    vm = pltpu.VMEM
    any_spec = pl.BlockSpec(memory_space=pl.ANY)
    vm_spec = pl.BlockSpec(memory_space=vm)
    outs = (
        ((BLK, KVC), BF),
        ((BLK, 128), F32),
        ((BLK, 128), F32),
        ((1, TOK, INNER), BF),
        ((1, TOK, D), BF),
        ((1, BLK, INNER), BF),
    )
    given = (plan.reshape(8, 128), local_params, master, momentum, inner_weight, activations, out_grad)
    results = pl.pallas_call(
        kernel,
        out_shape=tuple(vm(*out) for out in outs),
        in_specs=[any_spec] * 7,
        out_specs=[vm_spec] * 6,
        scratch_shapes=[
            vm((8, 128), jnp.int32),
            vm((BLK, 128), F32),
            vm((2, 2, QR, KVC), BF),
            vm((2, 2, 4, 2, HALF, 128), BF),
            vm((2, 4, 2, HALF, 128), BF),
            vm((2, 2, HALF, 128), BF),
            vm((2, 2, 2, HALF, 128), BF),
            vm((2, HALF, 128), BF),
            vm((2, 2, 4, 2, HALF, 128), BF),
            vm((2, BLK, 128), F32),
            vm((2, BLK, 128), F32),
            vm((TOK, D), BF),
            vm((TOK, INNER), BF),
            vm((4, TOK, BLK), BF),
            vm((TOK, INNER), BF),
            vm((D, INNER), BF),
            vm((4 * BLK, INNER), BF),
            vm((2, HALF, INNER), BF),
            vm((2, BLK, INNER), BF),
            vm((TOK, INNER), F32),
            pltpu.SemaphoreType.DMA((len(KEYS),)),
            pltpu.SemaphoreType.DMA((len(KEYS),)),
            pltpu.SemaphoreType.DMA((len(LOCAL),)),
            pltpu.SemaphoreType.REGULAR((6,)),
        ],
        compiler_params=pltpu.CompilerParams(
            collective_id=0, has_side_effects=True, vmem_limit_bytes=44 << 20
        ),
        cost_estimate=pl.CostEstimate(
            flops=6 * TOK * D * INNER, bytes_accessed=26 << 20, transcendentals=0
        ),
        name="sync_and_layer",
    )(*(pltpu.with_memory_space_constraint(a, pltpu.HBM) for a in given))
    return pl.pallas_call(
        write_out,
        out_shape=tuple(jax.ShapeDtypeStruct(*out) for out in outs),
        in_specs=[vm_spec] * 6,
        out_specs=[any_spec] * 6,
        scratch_shapes=[pltpu.SemaphoreType.DMA((6,))],
        compiler_params=pltpu.CompilerParams(vmem_limit_bytes=1 << 20),
        name="write_out",
    )(*(pltpu.with_memory_space_constraint(r, vm) for r in results))


def solution(mesh):
    placed = (
        P("shard"),
        P(None, "rep", "shard", None),
        P(None, "shard", "rep"),
        P(None, "shard", "rep"),
        P("rep", "shard", None),
        P("rep", "shard", None),
        P("rep", "shard", None),
    )
    return jax.shard_map(
        body,
        mesh=mesh,
        in_specs=placed,
        out_specs=(
            P("shard", None),
            P("shard", "rep"),
            P("shard", "rep"),
            P("rep", "shard", None),
            P("rep", "shard", None),
            P("rep", "shard", None),
        ),
        check_vma=False,
    )
```

```python
import jax
import jax.numpy as jnp
from jax import lax
from jax.experimental import pallas as pl
from jax.experimental.pallas import tpu as pltpu
from jax.sharding import PartitionSpec as P

OUTER_LR = 0.7
OUTER_MU = 0.9
BF = jnp.bfloat16
F32 = jnp.float32
D, KVC, INNER, TOK = 8192, 2048, 512, 256
BLK = 1024
QR = 256
HALF = 512
QS = range(4)
HS = range(2)

KEYS = (
    [("og",)]
    + [("ax", k) for k in range(4)]
    + [("g1", w, q) for w in "SUD" for q in QS]
    + [("g2", w, q) for w, qs in (("U", (0, 1)), ("D", (2, 3))) for q in qs]
    + [("g3", w, q) for w in "UD" for q in QS]
    + [("g4", q) for q in (1, 2)]
    + [("g5", w) for w in "UD"]
    + [("rb", w, i) for w in "UD" for i in HS]
    + [("rc", w, q) for w in "UD" for q in QS]
    + [("c1", h) for h in HS]
    + [("zb", w) for w in "UD"]
    + [("zc", w, h) for w in "UD" for h in HS]
    + [("xr", h) for h in HS]
    + [("xp", h) for h in HS]
    + [("zp", w, h) for w in "UD" for h in HS]
    + [("zf", w) for w in "UD"]
    + [("c2", k, h) for k in range(4) for h in HS]
)
SEM = {key: i for i, key in enumerate(KEYS)}
LATE = (("g4", 2), ("g5", "U"), ("g5", "D"), ("g3", "U", 2), ("g3", "D", 2))
LOCAL = (
    ["og", "plan", "w", "mast", "mom", "np"]
    + [("act", j) for j in range(8)]
    + [("lp", k) for k in QS]
)
LSEM = {key: i for i, key in enumerate(LOCAL)}


def kernel(
    plan_h, lp_h, mast_h, mom_h, w_h, act_h, og_h,
    np_o, nm, nmo, keys_o, ig, wg_o,
    plan_v, pick, lpb, sel, cr, zb, zc, xr, npv, mast, mom,
    act, og, acts, ogs, wg, tt, rb, rc, acc,
    ss, rs, ls, here,
):
    rep, shard = lax.axis_index("rep"), lax.axis_index("shard")
    z, xl, c = rep // 4, (rep // 2) % 2, rep % 2
    y, xh = shard // 2, shard % 2
    yu, yd, yo = (y + 1) % 4, (y + 3) % 4, (y + 2) % 4
    zu, zd, zo = (z + 1) % 4, (z + 3) % 4, (z + 2) % 4
    me, sib = shard, y * 2 + 1 - xh
    bu, bd, bo = yu * 2 + xh, yd * 2 + xh, yo * 2 + xh
    bus, bds, bos = yu * 2 + 1 - xh, yd * 2 + 1 - xh, yo * 2 + 1 - xh
    to = {
        "U": (rep, bu), "D": (rep, bd), "S": (rep, sib),
        "X": (z * 4 + (1 - xl) * 2 + c, shard), "C": (z * 4 + xl * 2 + 1 - c, shard),
        "ZU": (zu * 4 + xl * 2 + c, shard), "ZD": (zd * 4 + xl * 2 + c, shard),
    }
    started, late = [], []

    def remote(src, dst, key, way):
        return pltpu.make_async_remote_copy(
            src_ref=src, dst_ref=dst, send_sem=ss.at[SEM[key]], recv_sem=rs.at[SEM[key]],
            device_id=to[way], device_id_type=pl.DeviceIdType.MESH,
        )

    def send(src, dst, key, way):
        remote(src, dst, key, way).start()
        (late if key in LATE else started).append((src, dst, key, way))

    def arrived(dst, key, way):
        remote(dst, dst, key, way).wait_recv()

    def fetch(src, dst, key):
        copy = pltpu.make_async_copy(src, dst, ls.at[LSEM[key]])
        copy.start()
        return copy

    def rows(block, q=0, n=QR):
        return pl.ds(pl.multiple_of(block * BLK + q * QR, QR), n)

    def cols(block, i=0, n=BLK):
        return pl.ds(pl.multiple_of(block * BLK + i, QR), n)

    barrier = pltpu.get_barrier_semaphore()

    def signal(semaphore, way):
        pl.semaphore_signal(semaphore, inc=1, device_id=to[way], device_id_type=pl.DeviceIdType.MESH)

    before = {
        "U": y == 3, "D": y > 0, "S": xh == 1, "X": xl == 1, "ZU": z == 3, "ZD": z > 0,
    }
    back_of = {"U": "D", "D": "U", "S": "S", "X": "X", "ZU": "ZD", "ZD": "ZU"}
    slot = {way: i for i, way in enumerate(before)}
    signal(barrier, "C")
    for way, first in before.items():
        pl.when(jnp.logical_not(first))(lambda way=way: signal(barrier, way))
    expected = 1
    for first in before.values():
        expected = expected + jnp.where(first, 1, 0)
    pl.semaphore_wait(barrier, expected)
    for way, first in before.items():
        pl.when(first)(lambda way=way: signal(here.at[slot[back_of[way]]], way))

    def answered(way):
        pl.when(jnp.logical_not(before[way]))(lambda: pl.semaphore_wait(here.at[slot[way]], 1))

    def tokens(k):
        yy = (yo, yu, yd, y)[k]
        return act_h.at[0, :, cols(yy * 2 + 1 - xh)], acts.at[yy], ("ax", k), "S"

    def weight(w, q):
        return w_h.at[0, pl.ds(q * QR, QR)], wg.at[rows(me, q)], ("g1", w, q), w

    def tokens_to_sibling(k):
        send(*tokens(k))

    def weight_to_sibling(q):
        send(*weight("S", q))

    def first_copies(way):
        if way == "S":
            return [(og_h.at[0], ogs, ("og",), "S")] + [tokens(k) for k in range(3)]
        return [weight(way, q) for q in ((0, 1, 2, 3) if way == "U" else (3, 2, 1, 0))]

    def first_sends(way):
        for copy in first_copies(way):
            remote(*copy).start()

    for way in ("U", "D", "S"):
        pl.when(before[way])(lambda way=way: first_sends(way))
    for way in ("U", "S", "D"):

        @pl.when(jnp.logical_not(before[way]))
        def _(way=way):
            pl.semaphore_wait(here.at[slot[way]], 1)
            first_sends(way)

        started.extend(first_copies(way))

    f_plan = fetch(plan_h, plan_v, "plan")
    f_lp = [
        fetch(lp_h.at[:, 0, pl.ds(k * QR, QR)], lpb.at[k % 2], ("lp", k)) for k in (0, 1)
    ]
    f_og = fetch(og_h.at[0], og, "og")
    f_w = fetch(w_h.at[0], wg.at[rows(me, 0, BLK)], "w")
    order = [me, bo, bu, bd, bus, bds, bos, sib]
    f_act = [fetch(act_h.at[0, :, cols(j)], act.at[:, cols(j)], ("act", i)) for i, j in enumerate(order)]
    f_mast = fetch(mast_h, mast, "mast")
    f_mom = fetch(mom_h, mom, "mom")


    f_plan.wait()
    for g in range(8):
        line = plan_v[pl.ds(g, 1), :].astype(F32)
        pick[pl.ds(g * 128, 128), :] = jnp.broadcast_to(line, (128, 128)).T

    for k in QS:
        f_lp[k].wait()

        def choose(i, _, k=k):
            r = pl.multiple_of(i * 64, 64)
            mask = pick[pl.ds(k * QR + r, 64), :] == 1.0
            for b in range(16):
                a0 = lpb[k % 2, 0, pl.ds(r, 64), b * 128 : (b + 1) * 128].astype(F32)
                a1 = lpb[k % 2, 1, pl.ds(r, 64), b * 128 : (b + 1) * 128].astype(F32)
                sel[b % 2, k // 2, b // 4, (b // 2) % 2, pl.ds((k % 2) * QR + r, 64), :] = jnp.where(
                    mask, a1, a0
                ).astype(BF)
            return 0

        lax.fori_loop(0, 4, choose, 0)
        if k < 2:
            f_lp.append(
                fetch(lp_h.at[:, 0, pl.ds((k + 2) * QR, QR)], lpb.at[k % 2], ("lp", k + 2))
            )
        if k % 2 == 1:
            send(sel.at[1 - c, k // 2], cr.at[k // 2], ("c1", k // 2), "C")

    f_og.wait()
    acc[...] = jnp.zeros_like(acc)

    def layer(block, q0=0, n=4):
        def sub(i, _):
            at = cols(block, (q0 + i) * QR, QR)
            w = wg[at, :]
            acc[...] += jnp.dot(act[:, at], w, preferred_element_type=F32)
            ig[0, :, at] = lax.dot_general(
                og[...], w, (((1,), (1,)), ((), ())), preferred_element_type=F32
            ).astype(BF)
            return 0

        lax.fori_loop(0, n, sub, 0)

    def term(k, each=None):
        yy = (yo, yu, yd, y)[k]
        arrived(acts.at[yy], ("ax", k), "S")
        if k == 0:
            weight_to_sibling(0)

        def sub(i, _):
            at = pl.ds(pl.multiple_of(i * QR, QR), QR)
            over_tokens = (((0,), (0,)), ((), ()))
            t = lax.dot_general(
                act[:, cols(yy * 2 + xh, i * QR, QR)], og[...], over_tokens, preferred_element_type=F32
            ) + lax.dot_general(acts[yy, :, at], ogs[...], over_tokens, preferred_element_type=F32)
            tt[rows(yy, i), :] = t.astype(BF)
            return 0

        if each is None:
            lax.fori_loop(0, 4, sub, 0)
        else:
            for q in (0, 2, 1, 3):
                lax.fori_loop(q, q + 1, sub, 0)
                each(q)

    def add_into(dst, dst_row, *sources):
        def sub(i, _):
            at = pl.ds(pl.multiple_of(dst_row + i * 64, 64), 64)
            total = dst[at, :].astype(F32)
            for ref, row in sources:
                total = total + ref[pl.ds(row + i * 64, 64), :].astype(F32)
            dst[at, :] = total.astype(BF)
            return 0

        lax.fori_loop(0, QR // 64, sub, 0)

    f_w.wait()
    for copy in f_act:
        copy.wait()
    layer(me)

    def core_sum(zz, h):
        def sub(i, _):
            at = pl.ds(pl.multiple_of(i * 128, 128), 128)
            for l in HS:
                sel[c, h, zz, l, at, :] = (
                    sel[c, h, zz, l, at, :].astype(F32) + cr[h, zz, l, at, :].astype(F32)
                ).astype(BF)
            return 0

        lax.fori_loop(0, 4, sub, 0)

    for h in HS:
        arrived(cr.at[h], ("c1", h), "C")
    core_sum(zo, 0)
    answered("ZU")
    answered("ZD")
    send(sel.at[c, 0, zo], zb.at[1], ("zb", "D"), "ZD")
    core_sum(zo, 1)
    send(sel.at[c, 1, zo], zb.at[0], ("zb", "U"), "ZU")
    core_sum(zu, 0)
    send(sel.at[c, 0, zu], zc.at[0, 0], ("zc", "U", 0), "ZU")
    core_sum(zd, 1)
    send(sel.at[c, 1, zd], zc.at[1, 1], ("zc", "D", 1), "ZD")
    core_sum(zu, 1)
    core_sum(zd, 0)
    core_sum(z, 0)
    core_sum(z, 1)

    for q in (0, 1):
        arrived(wg.at[rows(bd, q)], ("g1", "U", q), "D")
        send(wg.at[rows(bd, q)], wg.at[rows(bd, q)], ("g2", "U", q), "U")
        arrived(wg.at[rows(bu, 3 - q)], ("g1", "D", 3 - q), "U")
        send(wg.at[rows(bu, 3 - q)], wg.at[rows(bu, 3 - q)], ("g2", "D", 3 - q), "D")

    arrived(ogs, ("og",), "S")
    def far_block(q):
        way = "D" if q < 2 else "U"
        side = 1 if q < 2 else 0
        send(tt.at[rows(yo, q)], rb.at[side, pl.ds((q % 2) * QR, QR)], ("rb", way, q % 2), way)

    term(0, far_block)

    def z_add(h, zz, way):
        def sub(i, _):
            at = pl.ds(pl.multiple_of(i * 128, 128), 128)
            for l in HS:
                sel[c, h, zz, l, at, :] = (
                    sel[c, h, zz, l, at, :].astype(F32) + zb[way, l, at, :].astype(F32)
                ).astype(BF)
            return 0

        lax.fori_loop(0, 4, sub, 0)

    arrived(zb.at[0], ("zb", "U"), "ZD")
    z_add(1, zu, 0)
    send(sel.at[c, 1, zu], zc.at[0, 1], ("zc", "U", 1), "ZU")
    arrived(zb.at[1], ("zb", "D"), "ZU")
    z_add(0, zd, 1)
    send(sel.at[c, 0, zd], zc.at[1, 0], ("zc", "D", 0), "ZD")

    term(1)
    for q in (0, 1):
        send(tt.at[rows(yu, q)], rc.at[0, pl.ds(q * QR, QR)], ("rc", "U", q), "U")

    answered("X")
    for h in HS:
        arrived(zc.at[0, h], ("zc", "U", h), "ZD")
        arrived(zc.at[1, h], ("zc", "D", h), "ZU")

        def z_sum(i, _, h=h):
            at = pl.ds(pl.multiple_of(i * 128, 128), 128)
            sel[c, h, z, 1 - xl, at, :] = (
                sel[c, h, z, 1 - xl, at, :].astype(F32)
                + zc[0, h, 1 - xl, at, :].astype(F32)
                + zc[1, h, 1 - xl, at, :].astype(F32)
            ).astype(BF)
            return 0

        lax.fori_loop(0, 4, z_sum, 0)
        send(sel.at[c, h, z, 1 - xl], xr.at[h], ("xr", h), "X")

    weight_to_sibling(3)
    for q in (2, 3):
        arrived(wg.at[rows(bd, q)], ("g1", "U", q), "D")
        arrived(wg.at[rows(bu, 3 - q)], ("g1", "D", 3 - q), "U")
    layer(bd)
    layer(bu)

    term(2)
    for q in (2, 3):
        send(tt.at[rows(yd, q)], rc.at[1, pl.ds(q * QR, QR)], ("rc", "D", q), "D")

    for i in HS:
        q = 2 + i
        arrived(rb.at[0, pl.ds(i * QR, QR)], ("rb", "U", i), "D")
        add_into(tt, yu * BLK + q * QR, (rb.at[0], i * QR))
        send(tt.at[rows(yu, q)], rc.at[0, pl.ds(q * QR, QR)], ("rc", "U", q), "U")
        arrived(rb.at[1, pl.ds(i * QR, QR)], ("rb", "D", i), "U")
        add_into(tt, yd * BLK + i * QR, (rb.at[1], i * QR))
        send(tt.at[rows(yd, i)], rc.at[1, pl.ds(i * QR, QR)], ("rc", "D", i), "D")

    f_mast.wait()
    f_mom.wait()
    for h in HS:
        arrived(xr.at[h], ("xr", h), "X")

        def update(i, _, h=h):
            at = pl.ds(pl.multiple_of(i * 64, 64), 64)
            to_row = pl.ds(pl.multiple_of(h * HALF + i * 64, 64), 64)
            total = (
                sel[c, h, z, xl, at, :].astype(F32)
                + zc[0, h, xl, at, :].astype(F32)
                + zc[1, h, xl, at, :].astype(F32)
                + xr[h, at, :].astype(F32)
            )
            mask = pick[to_row, :] == 1.0
            master_now = jnp.where(mask, mast[1, to_row, :], mast[0, to_row, :])
            moment_now = jnp.where(mask, mom[1, to_row, :], mom[0, to_row, :])
            outer_grad = master_now - total / 16
            new_momentum = OUTER_MU * moment_now + outer_grad
            new_master = master_now - OUTER_LR * (outer_grad + OUTER_MU * new_momentum)
            nmo[to_row, :] = new_momentum
            nm[to_row, :] = new_master
            npv[c, h, z, xl, at, :] = new_master.astype(BF)
            return 0

        lax.fori_loop(0, 8, update, 0)
        send(npv.at[c, h, z, xl], npv.at[c, h, z, xl], ("xp", h), "X")

    for q in (1, 2):
        weight_to_sibling(q)
    tokens_to_sibling(3)

    for q in QS:
        way, back = ("U", "D") if q < 2 else ("D", "U")
        arrived(wg.at[rows(bo, q)], ("g2", way, q), back)
        if q in (1, 2):
            send(wg.at[rows(bo, q)], wg.at[rows(bo, q)], ("g4", q), "S")
    layer(bo)

    def pass_on(q):
        arrived(wg.at[rows(sib, q)], ("g1", "S", q), "S")
        for w in "UD":
            send(wg.at[rows(sib, q)], wg.at[rows(sib, q)], ("g3", w, q), w)

    pass_on(0)

    for h in HS:
        arrived(npv.at[c, h, z, 1 - xl], ("xp", h), "X")
        for w in "UD":
            send(npv.at[c, h, z], npv.at[c, h, z], ("zp", w, h), "Z" + w)
        send(npv.at[c, h, z], npv.at[c, h, z], ("c2", 0, h), "C")

    for h in HS:
        pass_on((3, 1)[h])
        arrived(npv.at[c, h, zd], ("zp", "U", h), "ZD")
        if h == 0:
            send(npv.at[c, 0, zd], npv.at[c, 0, zd], ("zf", "U"), "ZU")
        send(npv.at[c, h, zd], npv.at[c, h, zd], ("c2", 1, h), "C")
        arrived(npv.at[c, h, zu], ("zp", "D", h), "ZU")
        if h == 1:
            send(npv.at[c, 1, zu], npv.at[c, 1, zu], ("zf", "D"), "ZD")
        send(npv.at[c, h, zu], npv.at[c, h, zu], ("c2", 2, h), "C")
    pass_on(2)

    arrived(wg.at[rows(bds, 0)], ("g3", "U", 0), "D")
    send(wg.at[rows(bds, 0)], wg.at[rows(bds, 0)], ("g5", "U"), "U")
    arrived(wg.at[rows(bus, 3)], ("g3", "D", 3), "U")
    send(wg.at[rows(bus, 3)], wg.at[rows(bus, 3)], ("g5", "D"), "D")

    arrived(npv.at[c, 0, zo], ("zf", "U"), "ZD")
    send(npv.at[c, 0, zo], npv.at[c, 0, zo], ("c2", 3, 0), "C")
    arrived(npv.at[c, 1, zo], ("zf", "D"), "ZU")
    send(npv.at[c, 1, zo], npv.at[c, 1, zo], ("c2", 3, 1), "C")

    layer(sib)

    term(3)
    for q in QS:
        arrived(rc.at[0, pl.ds(q * QR, QR)], ("rc", "U", q), "D")
        arrived(rc.at[1, pl.ds(q * QR, QR)], ("rc", "D", q), "U")

        def grad_sum(i, _, q=q):
            at = pl.ds(pl.multiple_of(q * QR + i * 64, 64), 64)
            wg_o[0, at, :] = (
                tt[pl.ds(pl.multiple_of(y * BLK + q * QR + i * 64, 64), 64), :].astype(F32)
                + rc[0, at, :].astype(F32)
                + rc[1, at, :].astype(F32)
            ).astype(BF)
            return 0

        lax.fori_loop(0, 4, grad_sum, 0)

    for h in HS:
        for k, zz in enumerate((z, zd, zu, zo)):
            arrived(npv.at[1 - c, h, zz], ("c2", k, h), "C")
    for b in range(16):
        for h in HS:
            pltpu.make_async_copy(
                npv.at[b % 2, h, b // 4, (b // 2) % 2],
                np_o.at[pl.ds(h * HALF, HALF), pl.ds(b * 128, 128)],
                ls.at[LSEM["np"]],
            ).start()

    layer(bds, 0, 1)
    layer(bus, 3, 1)
    arrived(wg.at[rows(bds, 3)], ("g3", "U", 3), "D")
    layer(bds, 3, 1)
    arrived(wg.at[rows(bus, 0)], ("g3", "D", 0), "U")
    layer(bus, 0, 1)
    pltpu.make_async_copy(np_o, np_o, ls.at[LSEM["np"]]).wait()
    for q in (1, 2):
        arrived(wg.at[rows(bds, q)], ("g3", "U", q), "D")
        layer(bds, q, 1)
        arrived(wg.at[rows(bus, q)], ("g3", "D", q), "U")
        layer(bus, q, 1)
    arrived(wg.at[rows(bos, 1)], ("g4", 1), "S")
    layer(bos, 1, 1)
    for copy in started:
        remote(*copy).wait_send()
    arrived(wg.at[rows(bos, 0)], ("g5", "U"), "D")
    layer(bos, 0, 1)
    arrived(wg.at[rows(bos, 3)], ("g5", "D"), "U")
    layer(bos, 3, 1)
    arrived(wg.at[rows(bos, 2)], ("g4", 2), "S")
    layer(bos, 2, 1)
    keys_o[0] = acc[...].astype(BF)
    for copy in late:
        remote(*copy).wait_send()


def write_out(*refs):
    n = len(refs) // 2
    sems = refs[-1]
    copies = [pltpu.make_async_copy(refs[i], refs[n + i], sems.at[i]) for i in range(n)]
    for copy in copies:
        copy.start()
    for copy in copies:
        copy.wait()


def body(plan, local_params, master, momentum, inner_weight, activations, out_grad):
    vm = pltpu.VMEM
    any_spec = pl.BlockSpec(memory_space=pl.ANY)
    vm_spec = pl.BlockSpec(memory_space=vm)
    outs = (
        ((BLK, KVC), BF),
        ((BLK, 128), F32),
        ((BLK, 128), F32),
        ((1, TOK, INNER), BF),
        ((1, TOK, D), BF),
        ((1, BLK, INNER), BF),
    )
    given = (plan.reshape(8, 128), local_params, master, momentum, inner_weight, activations, out_grad)
    results = pl.pallas_call(
        kernel,
        out_shape=tuple(vm(*out) for out in outs),
        in_specs=[any_spec] * 7,
        out_specs=[vm_spec] * 6,
        scratch_shapes=[
            vm((8, 128), jnp.int32),
            vm((BLK, 128), F32),
            vm((2, 2, QR, KVC), BF),
            vm((2, 2, 4, 2, HALF, 128), BF),
            vm((2, 4, 2, HALF, 128), BF),
            vm((2, 2, HALF, 128), BF),
            vm((2, 2, 2, HALF, 128), BF),
            vm((2, HALF, 128), BF),
            vm((2, 2, 4, 2, HALF, 128), BF),
            vm((2, BLK, 128), F32),
            vm((2, BLK, 128), F32),
            vm((TOK, D), BF),
            vm((TOK, INNER), BF),
            vm((4, TOK, BLK), BF),
            vm((TOK, INNER), BF),
            vm((D, INNER), BF),
            vm((4 * BLK, INNER), BF),
            vm((2, HALF, INNER), BF),
            vm((2, BLK, INNER), BF),
            vm((TOK, INNER), F32),
            pltpu.SemaphoreType.DMA((len(KEYS),)),
            pltpu.SemaphoreType.DMA((len(KEYS),)),
            pltpu.SemaphoreType.DMA((len(LOCAL),)),
            pltpu.SemaphoreType.REGULAR((6,)),
        ],
        compiler_params=pltpu.CompilerParams(
            collective_id=0, has_side_effects=True, vmem_limit_bytes=44 << 20
        ),
        cost_estimate=pl.CostEstimate(
            flops=6 * TOK * D * INNER, bytes_accessed=26 << 20, transcendentals=0
        ),
        name="sync_and_layer",
    )(*(pltpu.with_memory_space_constraint(a, pltpu.HBM) for a in given))
    return pl.pallas_call(
        write_out,
        out_shape=tuple(jax.ShapeDtypeStruct(*out) for out in outs),
        in_specs=[vm_spec] * 6,
        out_specs=[any_spec] * 6,
        scratch_shapes=[pltpu.SemaphoreType.DMA((6,))],
        compiler_params=pltpu.CompilerParams(vmem_limit_bytes=1 << 20),
        name="write_out",
    )(*(pltpu.with_memory_space_constraint(r, vm) for r in results))


def solution(mesh):
    placed = (
        P("shard"),
        P(None, "rep", "shard", None),
        P(None, "shard", "rep"),
        P(None, "shard", "rep"),
        P("rep", "shard", None),
        P("rep", "shard", None),
        P("rep", "shard", None),
    )
    return jax.shard_map(
        body,
        mesh=mesh,
        in_specs=placed,
        out_specs=(
            P("shard", None),
            P("shard", "rep"),
            P("shard", "rep"),
            P("rep", "shard", None),
            P("rep", "shard", None),
            P("rep", "shard", None),
        ),
        check_vma=False,
    )
```
